32 devices in a mesh: shard: 8 (over z, y), tensor: 4 (over x, core).
Axes of the slice: x: 2, y: 2, z: 4, core: 2. Of those that a mesh axis runs over, the one named last changes fastest.
Arguments:
- grad_query: bfloat16 [8, 1024, 512], P('shard', None, 'tensor'), may hold values from -8 to 8
- error_query: float32 [8, 1024, 512], P('shard', None, 'tensor'), may hold values from -3 to 3
- grad_output: bfloat16 [8, 512, 1024], P('shard', 'tensor'), may hold values from -8 to 8
- error_output: float32 [8, 512, 1024], P('shard', 'tensor'), may hold values from -3 to 3
- start_query: float32 [512, 32], P('tensor'), may hold values from -6 to 6
- start_output: float32 [1024, 32], replicated, may hold values from -6 to 6
- weight_query: float32 [1024, 512], P('shard', 'tensor'), may hold values from -0.1875 to 0.1875
- weight_output: float32 [512, 1024], P('tensor', 'shard'), may hold values from -0.25 to 0.25
- moment_query: float32 [1024, 512], P('shard', 'tensor'), may hold values from -1.2 to 1.2
- moment_output: float32 [512, 1024], P('tensor', 'shard'), may hold values from -1.2 to 1.2
- grad_vector: bfloat16 [8, 3584], P('shard'), may hold values from -12 to 12
- moment_vector: float32 [3584], P('shard'), may hold values from -1.2 to 1.2
- weight_vector: float32 [3584], P('shard'), may hold values from 0.5 to 1.5
Outputs:
- new_error_query: float32 [8, 1024, 512], P('shard', None, 'tensor')
- new_error_output: float32 [8, 512, 1024], P('shard', 'tensor')
- new_moment_query: float32 [1024, 512], P('shard', 'tensor')
- new_moment_output: float32 [512, 1024], P('tensor', 'shard')
- new_weight_query: float32 [1024, 512], P(None, 'tensor')
- new_weight_output: float32 [512, 1024], P('tensor')
- new_moment_vector: float32 [3584], P('shard')
- new_weight_vector: float32 [3584], replicated
The draws below stay inside these ranges and needn't reach their ends.
All inputs are finite; a program needn't handle non-finite values.
Results may differ from the reference program's by a relative error of at most 0.0003.
Values sent between devices are 32-bit elements; how exact they have to be, the bound alone decides.
A program may use at most 64 MiB of HBM per device.

```python
import jax
import jax.numpy as jnp
from jax import lax

D = 1024
RANK = 32
ROUNDS = 2
HW = 512
VEC = 3584
REPL = 8
N_SHARD = 8


def shared_gradient(key, replicas, height, breadth):
    common = jax.random.normal(jax.random.fold_in(key, 11), (height, breadth), jnp.float32)
    single = jax.random.normal(jax.random.fold_in(key, 12), (replicas, height, breadth), jnp.float32)
    return jnp.clip(common[None] + single, -8.0, 8.0)


def draw_grad_query(key, part):
    return shared_gradient(jax.random.fold_in(key, 1), REPL, D, HW).astype(jnp.bfloat16)


def draw_grad_output(key, part):
    return shared_gradient(jax.random.fold_in(key, 2), REPL, HW, D).astype(jnp.bfloat16)


def steps_of(key, shape, pieces, least, largest):
    factor_of, own = 1.0, jax.random.fold_in(key, 6)
    for position, parts in pieces:
        steps = jnp.exp(jax.random.uniform(jax.random.fold_in(own, position), (parts,), jnp.float32, least / len(pieces), largest / len(pieces)))
        factor_of = factor_of * jnp.repeat(steps, shape[position] // parts).reshape([-1 if axis == position else 1 for axis in range(len(shape))])
    return factor_of


def normal_values(rng, dims, width, limit, pieces=(), kind=jnp.bfloat16):
    array = width * jax.random.normal(rng, dims, jnp.float32)
    if pieces:
        array = array * steps_of(rng, dims, pieces, -0.22, 0.18)
    return jnp.clip(array, -limit, limit).astype(kind)


def setup_inputs(seed: int = 0) -> dict:
    key_of = jax.random.split(jax.random.key(seed), 14)
    grad_query = draw_grad_query(jax.random.fold_in(key_of[13], 71), 0)
    error_query = normal_values(key_of[1], (REPL, D, HW), 0.5, 3.0, ((0, 8), (2, 4)), jnp.float32)
    grad_output = draw_grad_output(jax.random.fold_in(key_of[13], 71), 0)
    error_output = normal_values(key_of[3], (REPL, HW, D), 0.5, 3.0, ((0, 8), (1, 4)), jnp.float32)
    start_query = normal_values(key_of[4], (HW, RANK), 1.0, 6.0, ((0, 4),), jnp.float32)
    start_output = normal_values(key_of[5], (D, RANK), 1.0, 6.0, (), jnp.float32)
    weight_query = normal_values(key_of[6], (D, HW), D ** -0.5, 0.1875, ((0, 8), (1, 4)), jnp.float32)
    weight_output = normal_values(key_of[7], (HW, D), HW ** -0.5, 0.25, ((0, 4), (1, 8)), jnp.float32)
    moment_query = normal_values(key_of[8], (D, HW), 0.2, 1.2, ((0, 8), (1, 4)), jnp.float32)
    moment_output = normal_values(key_of[9], (HW, D), 0.2, 1.2, ((0, 4), (1, 8)), jnp.float32)
    grad_vector = normal_values(key_of[10], (REPL, VEC), 2.0, 12.0, ((0, 8),))
    moment_vector = normal_values(key_of[11], (VEC,), 0.2, 1.2, ((0, 8),), jnp.float32)
    weight_vector = jnp.clip(1.0 + 0.1 * jax.random.normal(key_of[12], (VEC,), jnp.float32), 0.5, 1.5)
    return {"grad_query": grad_query, "error_query": error_query, "grad_output": grad_output, "error_output": error_output, "start_query": start_query, "start_output": start_output, "weight_query": weight_query, "weight_output": weight_output, "moment_query": moment_query, "moment_output": moment_output, "grad_vector": grad_vector, "moment_vector": moment_vector, "weight_vector": weight_vector}


def orthonormal(factor):
    gram = jnp.dot(factor.T.astype(jnp.float32), factor.astype(jnp.float32), precision=lax.Precision.HIGHEST, preferred_element_type=jnp.float32)
    lower = jnp.linalg.cholesky(gram)
    return jax.scipy.linalg.solve_triangular(lower, factor.T, lower=True).T

def reference(grad_query, error_query, grad_output, error_output, start_query, start_output, weight_query, weight_output, moment_query, moment_output, grad_vector, moment_vector, weight_vector):
    highest = lax.Precision.HIGHEST
    total_query = grad_query.astype(jnp.float32) + error_query
    total_output = grad_output.astype(jnp.float32) + error_output
    factor_query = start_query
    factor_output = start_output
    for turn in range(ROUNDS):
        left_query = orthonormal(jnp.einsum('rij,jk->ik', total_query, factor_query, precision=highest))
        factor_query = jnp.einsum('rij,ik->jk', total_query, left_query, precision=highest)
        left_output = orthonormal(jnp.einsum('rij,jk->ik', total_output, factor_output, precision=highest))
        factor_output = jnp.einsum('rij,ik->jk', total_output, left_output, precision=highest)
    approx_query = jnp.dot(left_query.astype(jnp.float32), factor_query.T.astype(jnp.float32), precision=highest, preferred_element_type=jnp.float32) / N_SHARD
    approx_output = jnp.dot(left_output.astype(jnp.float32), factor_output.T.astype(jnp.float32), precision=highest, preferred_element_type=jnp.float32) / N_SHARD
    new_error_query = total_query - approx_query[None]
    new_error_output = total_output - approx_output[None]
    new_moment_query = 0.9 * moment_query + approx_query
    new_moment_output = 0.9 * moment_output + approx_output
    new_weight_query = weight_query - 0.01 * new_moment_query
    new_weight_output = weight_output - 0.01 * new_moment_output
    vector_mean = jnp.sum(grad_vector.astype(jnp.float32), axis=0) / N_SHARD
    new_moment_vector = 0.9 * moment_vector + vector_mean
    new_weight_vector = weight_vector - 0.01 * new_moment_vector
    return (new_error_query, new_error_output, new_moment_query, new_moment_output, new_weight_query, new_weight_output, new_moment_vector, new_weight_vector)
```

```python
import jax
import jax.numpy as jnp
from jax import lax
from jax.experimental import pallas as pl
from jax.experimental.pallas import tpu as pltpu
from jax.sharding import PartitionSpec as P

ROUNDS = 2


highest = lax.Precision.HIGHEST


def product(left, right):
    return jnp.dot(left, right, precision=highest, preferred_element_type=jnp.float32)


def product_inner(left, right):
    return lax.dot_general(
        left, right, (((0,), (0,)), ((), ())), precision=highest, preferred_element_type=jnp.float32
    )


def solve_rows(gram, factor):
    lower = jnp.linalg.cholesky(gram)
    return jax.scipy.linalg.solve_triangular(lower, factor.T, lower=True).T


def orthonormal(factor):
    return solve_rows(product_inner(factor, factor), factor)


def orthonormal_rows(factor):
    gram = lax.psum(product_inner(factor, factor), "tensor")
    return solve_rows(gram, factor)


def local(
    grad_query,
    error_query,
    grad_output,
    error_output,
    start_query,
    start_output,
    weight_query,
    weight_output,
    moment_query,
    moment_output,
    grad_vector,
    moment_vector,
    weight_vector,
):
    replicas = lax.axis_size("shard")
    shard_index = lax.axis_index("shard")
    total_query = grad_query[0].astype(jnp.float32) + error_query[0]
    total_output = grad_output[0].astype(jnp.float32) + error_output[0]
    factor_query = start_query
    factor_output = start_output
    for turn in range(ROUNDS):
        part_query = product(total_query, factor_query)
        part_output = product(total_output, factor_output)
        sum_query = lax.psum(part_query, ("shard", "tensor"))
        sum_output = lax.psum(part_output, "shard")
        left_query = orthonormal(sum_query)
        left_output = orthonormal_rows(sum_output)
        right_query_part = product_inner(total_query, left_query)
        right_output_part = product_inner(total_output, left_output)
        factor_query = lax.psum(right_query_part, "shard")
        factor_output = lax.psum(right_output_part, ("shard", "tensor"))
    approx_query = product(left_query, factor_query.T) / replicas
    approx_output = product(left_output, factor_output.T) / replicas
    new_error_query = (total_query - approx_query)[None]
    new_error_output = (total_output - approx_output)[None]
    rows_block = moment_query.shape[0]
    block_query = lax.dynamic_slice_in_dim(approx_query, shard_index * rows_block, rows_block, 0)
    cols_block = moment_output.shape[1]
    block_output = lax.dynamic_slice_in_dim(approx_output, shard_index * cols_block, cols_block, 1)
    new_moment_query = 0.9 * moment_query + block_query
    new_moment_output = 0.9 * moment_output + block_output
    stepped_query = weight_query - 0.01 * new_moment_query
    stepped_output = weight_output - 0.01 * new_moment_output
    local_vector = grad_vector[0].astype(jnp.float32)
    vector_block = moment_vector.shape[0]
    vector_whole = lax.psum(local_vector, "shard")
    vector_part = lax.dynamic_slice_in_dim(
        vector_whole, shard_index * vector_block, vector_block, 0
    )
    vector_mean = vector_part / replicas
    new_moment_vector = 0.9 * moment_vector + vector_mean
    stepped_vector = weight_vector - 0.01 * new_moment_vector
    new_weight_query, new_weight_output, new_weight_vector = (
        lax.all_gather(stepped_query, "shard", axis=0, tiled=True),
        lax.all_gather(stepped_output, "shard", axis=1, tiled=True),
        lax.all_gather(stepped_vector, "shard", axis=0, tiled=True),
    )
    return (
        new_error_query,
        new_error_output,
        new_moment_query,
        new_moment_output,
        new_weight_query,
        new_weight_output,
        new_moment_vector,
        new_weight_vector,
    )


Z, Y, TENSOR = 4, 2, 4
SHARD = Z * Y
RANK = 32
B = 128
VEC_PAD = 512
SLOTS = 128
f32 = jnp.float32


def nn(left, right):
    return lax.dot_general(left, right, (((1,), (0,)), ((), ())), precision=highest, preferred_element_type=f32)


def nt(left, right):
    return lax.dot_general(left, right, (((1,), (1,)), ((), ())), precision=highest, preferred_element_type=f32)


def inverse_lower(gram):
    row = lax.broadcasted_iota(jnp.int32, (RANK, RANK), 0)
    lane = lax.broadcasted_iota(jnp.int32, (RANK, RANK), 1)
    left, right = gram, (row == lane).astype(f32)
    row_of = lax.broadcasted_iota(jnp.int32, (RANK, 1), 0)
    for k in range(RANK):
        ratio = jnp.where(row_of > k, left[:, k : k + 1] * (1.0 / left[k : k + 1, k : k + 1]), 0.0)
        left, right = left - ratio * left[k : k + 1, :], right - ratio * right[k : k + 1, :]
    diagonal = jnp.sum(jnp.where(row == lane, left, 0.0), axis=1, keepdims=True)
    return right * lax.rsqrt(diagonal)


def kernel(
    grad_q, error_q, grad_o, error_o, start_q, start_o, weight_q, weight_o, moment_q, moment_o,
    grad_v, moment_v, weight_v,
    new_error_q, new_error_o, new_moment_q, new_moment_o, new_weight_q, new_weight_o, new_moment_v, new_weight_v,
    tot, yrecv, zrecv, blk, wall, xq, xo, scat, got, gath, pall, fall, vpart, vrecv, vall,
    send_sem, recv_sem,
):
    s, t = lax.axis_index("shard"), lax.axis_index("tensor")
    z, y = s // Y, s % Y
    barrier = pltpu.get_barrier_semaphore()
    for k in range(1, SHARD):
        pl.semaphore_signal(barrier, inc=1, device_id=((s + k) % SHARD, t), device_id_type=pl.DeviceIdType.MESH)
    for k in range(1, TENSOR):
        pl.semaphore_signal(barrier, inc=1, device_id=(s, (t + k) % TENSOR), device_id_type=pl.DeviceIdType.MESH)

    used = [0]
    sent = []

    def copy(src, dst, device):
        slot = used[0]
        used[0] += 1
        out = pltpu.make_async_remote_copy(
            src_ref=src, dst_ref=dst, send_sem=send_sem.at[slot], recv_sem=recv_sem.at[slot],
            device_id=device, device_id_type=pl.DeviceIdType.MESH)
        out.start()
        sent.append(out)
        return slot

    def arrived(slot, buffer):
        pltpu.make_async_remote_copy(
            src_ref=buffer, dst_ref=buffer, send_sem=send_sem.at[slot], recv_sem=recv_sem.at[slot],
            device_id=(s, (t + 1) % TENSOR), device_id_type=pl.DeviceIdType.MESH).wait_recv()

    def spread_shard(buf):
        slots = [copy(buf.at[s], buf.at[s], ((s + k) % SHARD, t)) for k in range(1, SHARD)]

        def wait():
            for k, slot in enumerate(slots, 1):
                arrived(slot, buf.at[(s + SHARD - k) % SHARD])
        return wait

    def spread_tensor(buf):
        slots = [copy(buf.at[t], buf.at[t], (s, (t + k) % TENSOR)) for k in range(1, TENSOR)]

        def wait():
            for k, slot in enumerate(slots, 1):
                arrived(slot, buf.at[(t + TENSOR - k) % TENSOR])
        return wait

    def scatter_shard(src, dst):
        slots = [copy(src.at[(s + k) % SHARD], dst.at[k - 1], ((s + k) % SHARD, t)) for k in range(1, SHARD)]

        def wait():
            for k, slot in enumerate(slots, 1):
                arrived(slot, dst.at[k - 1])
        return wait

    for j in range(SHARD):
        tot[j, 0] = grad_q[j * B : (j + 1) * B, :].astype(f32) + error_q[j * B : (j + 1) * B, :]
        tot[j, 1] = grad_o[:, j * B : (j + 1) * B].astype(f32) + error_o[:, j * B : (j + 1) * B]
    pl.semaphore_wait(barrier, SHARD - 1 + TENSOR - 1)

    partner = (z * Y + 1 - y, t)
    order = [(z + k) % Z for k in (1, 2, 3, 0)]
    y_slots = [copy(tot.at[c * Y + 1 - y], yrecv.at[c], partner) for c in order]
    wall[s, 0] = weight_q[...] - 0.01 * (0.9 * moment_q[...])
    wall[s, 1] = weight_o[...] - 0.01 * (0.9 * moment_o[...])
    vec = grad_v[...].astype(f32)
    length = moment_v.shape[1]
    vpart[...] = jnp.zeros_like(vpart)
    vall[s] = jnp.zeros((1, VEC_PAD), f32)
    for j in range(SHARD):
        vpart[j, :, 0:length] = vec[:, j * length : (j + 1) * length]
    vector_wait = scatter_shard(vpart, vrecv)
    z_slots = []
    for c, slot in zip(order[:3], y_slots[:3]):
        arrived(slot, yrecv.at[c])
        yrecv[c] = yrecv[c] + tot[c * Y + y]
        z_slots.append(copy(yrecv.at[c], zrecv.at[len(z_slots)], (c * Y + y, t)))
    arrived(y_slots[3], yrecv.at[z])
    total = yrecv[z] + tot[s]
    w_slots = [copy(wall.at[s], wall.at[s], (((z + k) % Z) * Y + y, t)) for k in (1, 2, 3)]
    w_y_slots = [copy(wall.at[s], wall.at[s], partner)]

    def forward(k):
        c = ((z + Z - k) % Z) * Y + y
        arrived(w_slots[k - 1], wall.at[c])
        w_y_slots.append(copy(wall.at[c], wall.at[c], partner))

    for k, slot in enumerate(z_slots):
        arrived(slot, zrecv.at[k])
        total = total + zrecv[k]
    blk[...] = total

    vector_wait()
    vector_sum = vpart[s]
    for k in range(SHARD - 1):
        vector_sum = vector_sum + vrecv[k]
    moment = 0.9 * moment_v[...] + vector_sum[:, 0:length] / SHARD
    new_moment_v[...] = moment
    vall[s, :, 0:length] = weight_v[...] - 0.01 * moment
    vall_wait = spread_shard(vall)

    factor_q = start_q[...].T
    factor_o = start_o[pl.ds(pl.multiple_of(s * B, B), B), :].T
    inverse_q = inverse_o = None
    for turn in range(ROUNDS):
        last = turn == ROUNDS - 1
        a, b = 2 * turn, 2 * turn + 1
        part_o = nt(factor_o, blk[1])
        for j in range(RANK // 8):
            scat[a, j] = part_o[8 * j : 8 * j + 8]
            scat[a, j + RANK // 8] = jnp.zeros((8, B), f32)
        scat_wait = scatter_shard(scat.at[a], got.at[a])
        xq[turn, t] = nt(factor_q, blk[0])
        xq_wait = spread_tensor(xq.at[turn])
        if turn:
            inverse_q, inverse_o = inverse_lower(gram_q), inverse_lower(gram_o)
        xq_wait()
        left_q = xq[turn, 0] + xq[turn, 1] + xq[turn, 2] + xq[turn, 3]
        if turn:
            left_q = nn(inverse_q, left_q)
        right_q = nn(left_q, blk[0])
        square_q = nt(left_q, left_q)
        for j in range(RANK // 8):
            scat[b, j] = right_q[8 * j : 8 * j + 8]
            scat[b, j + RANK // 8] = jnp.zeros((8, B), f32)
            scat[b, j + RANK // 8, :, 0:RANK] = square_q[8 * j : 8 * j + 8]
        q_wait = scatter_shard(scat.at[b], got.at[b])
        scat_wait()
        piece = scat[a, s]
        for k in range(SHARD - 1):
            piece = piece + got[a, k]
        gath[a, s] = piece
        o_wait = spread_shard(gath.at[a])
        if last:
            pall[s] = left_q
            pall_wait = spread_shard(pall)
            forward(1)
        q_wait()
        piece = scat[b, s]
        for k in range(SHARD - 1):
            piece = piece + got[b, k]
        gath[b, s] = piece
        q_wait = spread_shard(gath.at[b])
        o_wait()
        left_o = gath[a, 0 : RANK // 8].reshape(RANK, B)
        if turn:
            left_o = nn(inverse_o, left_o)
        xo[turn, t, 0:RANK] = nn(left_o, blk[1])
        xo[turn, t, RANK : 2 * RANK] = jnp.zeros((RANK, B), f32)
        xo[turn, t, RANK : 2 * RANK, 0:RANK] = nt(left_o, left_o)
        xo_wait = spread_tensor(xo.at[turn])
        if last:
            forward(2)
        q_wait()
        factor_q = gath[b, 0 : RANK // 8].reshape(RANK, B)
        gram_q = gath[b, RANK // 8 : SHARD].reshape(RANK, B)[:, 0:RANK]
        xo_wait()
        both = xo[turn, 0] + xo[turn, 1] + xo[turn, 2] + xo[turn, 3]
        factor_o, gram_o = both[0:RANK], both[RANK : 2 * RANK, 0:RANK]

    fall[s] = factor_o
    fall_wait = spread_shard(fall)
    forward(3)
    inverse_q, inverse_o = inverse_lower(gram_q), inverse_lower(gram_o)
    side_q = nn(inverse_q.T, nn(inverse_q, factor_q)) / SHARD
    side_o = (nn(inverse_o.T, nn(inverse_o, left_o)) / SHARD).T
    new_moment_q[...] = 0.9 * moment_q[...] + nn(left_q.T, side_q)
    new_moment_o[...] = 0.9 * moment_o[...] + nn(side_o, factor_o)
    pall_wait()
    own = [(z + Z - k) % Z for k in (0, 1, 2, 3)]
    for c, slot in zip(own, w_y_slots):
        arrived(slot, wall.at[c * Y + 1 - y])
    for j in range(SHARD):
        approx = nn(pall[j].T, side_q)
        new_error_q[j * B : (j + 1) * B, :] = tot[j, 0] - approx
        new_weight_q[j * B : (j + 1) * B, :] = wall[j, 0] - 0.01 * approx
    fall_wait()
    for j in range(SHARD):
        approx = nn(side_o, fall[j])
        new_error_o[:, j * B : (j + 1) * B] = tot[j, 1] - approx
        new_weight_o[:, j * B : (j + 1) * B] = wall[j, 1] - 0.01 * approx
    vall_wait()
    new_weight_v[...] = vall[...]
    for out in sent:
        out.wait_send()


def fast_local(
    grad_query, error_query, grad_output, error_output, start_query, start_output, weight_query, weight_output,
    moment_query, moment_output, grad_vector, moment_vector, weight_vector,
):
    length = moment_vector.shape[0]
    vmem = pl.BlockSpec(memory_space=pltpu.VMEM)
    shape = lambda *dims: jax.ShapeDtypeStruct(dims, f32)
    scratch = lambda *dims: pltpu.VMEM(dims, f32)
    eq, eo, mq, mo, wq, wo, mv, wv = pl.pallas_call(
        kernel,
        out_shape=(
            shape(SHARD * B, B), shape(B, SHARD * B), shape(B, B), shape(B, B),
            shape(SHARD * B, B), shape(B, SHARD * B), shape(1, length), shape(SHARD, 1, VEC_PAD),
        ),
        in_specs=[vmem] * 13,
        out_specs=(vmem,) * 8,
        scratch_shapes=[
            scratch(SHARD, 2, B, B), scratch(Z, 2, B, B), scratch(Z - 1, 2, B, B), scratch(2, B, B),
            scratch(SHARD, 2, B, B), scratch(ROUNDS, TENSOR, RANK, B), scratch(ROUNDS, TENSOR, 2 * RANK, B),
            scratch(2 * ROUNDS, SHARD, 8, B), scratch(2 * ROUNDS, SHARD - 1, 8, B), scratch(2 * ROUNDS, SHARD, 8, B),
            scratch(SHARD, RANK, B), scratch(SHARD, RANK, B),
            scratch(SHARD, 1, VEC_PAD), scratch(SHARD - 1, 1, VEC_PAD), scratch(SHARD, 1, VEC_PAD),
            pltpu.SemaphoreType.DMA((SLOTS,)), pltpu.SemaphoreType.DMA((SLOTS,)),
        ],
        compiler_params=pltpu.CompilerParams(collective_id=0, has_side_effects=True, vmem_limit_bytes=40 * 2**20),
        cost_estimate=pl.CostEstimate(flops=2**30, bytes_accessed=5 * 2**20, transcendentals=0),
    )(
        grad_query[0], error_query[0], grad_output[0], error_output[0], start_query, start_output,
        weight_query, weight_output, moment_query, moment_output,
        grad_vector, moment_vector[None], weight_vector[None],
    )
    return eq[None], eo[None], mq, mo, wq, wo, mv[0], wv[:, 0, 0:length].reshape(-1)


def solution(mesh):
    in_specs = (
        P("shard", None, "tensor"),
        P("shard", None, "tensor"),
        P("shard", "tensor", None),
        P("shard", "tensor", None),
        P("tensor", None),
        P(),
        P("shard", "tensor"),
        P("tensor", "shard"),
        P("shard", "tensor"),
        P("tensor", "shard"),
        P("shard", None),
        P("shard"),
        P("shard"),
    )
    out_specs = (
        P("shard", None, "tensor"),
        P("shard", "tensor", None),
        P("shard", "tensor"),
        P("tensor", "shard"),
        P(None, "tensor"),
        P("tensor", None),
        P("shard"),
        P(),
    )
    body = fast_local if (mesh.shape["shard"], mesh.shape["tensor"]) == (Z * Y, TENSOR) else local
    return jax.shard_map(body, mesh=mesh, in_specs=in_specs, out_specs=out_specs, check_vma=False)
```

```python
import jax
import jax.numpy as jnp
from jax import lax
from jax.experimental import pallas as pl
from jax.experimental.pallas import tpu as pltpu
from jax.sharding import PartitionSpec as P

ROUNDS = 2


highest = lax.Precision.HIGHEST


def product(left, right):
    return jnp.dot(left, right, precision=highest, preferred_element_type=jnp.float32)


def product_inner(left, right):
    return lax.dot_general(
        left, right, (((0,), (0,)), ((), ())), precision=highest, preferred_element_type=jnp.float32
    )


def solve_rows(gram, factor):
    lower = jnp.linalg.cholesky(gram)
    return jax.scipy.linalg.solve_triangular(lower, factor.T, lower=True).T


def orthonormal(factor):
    return solve_rows(product_inner(factor, factor), factor)


def orthonormal_rows(factor):
    gram = lax.psum(product_inner(factor, factor), "tensor")
    return solve_rows(gram, factor)


def local(
    grad_query,
    error_query,
    grad_output,
    error_output,
    start_query,
    start_output,
    weight_query,
    weight_output,
    moment_query,
    moment_output,
    grad_vector,
    moment_vector,
    weight_vector,
):
    replicas = lax.axis_size("shard")
    shard_index = lax.axis_index("shard")
    total_query = grad_query[0].astype(jnp.float32) + error_query[0]
    total_output = grad_output[0].astype(jnp.float32) + error_output[0]
    factor_query = start_query
    factor_output = start_output
    for turn in range(ROUNDS):
        part_query = product(total_query, factor_query)
        part_output = product(total_output, factor_output)
        sum_query = lax.psum(part_query, ("shard", "tensor"))
        sum_output = lax.psum(part_output, "shard")
        left_query = orthonormal(sum_query)
        left_output = orthonormal_rows(sum_output)
        right_query_part = product_inner(total_query, left_query)
        right_output_part = product_inner(total_output, left_output)
        factor_query = lax.psum(right_query_part, "shard")
        factor_output = lax.psum(right_output_part, ("shard", "tensor"))
    approx_query = product(left_query, factor_query.T) / replicas
    approx_output = product(left_output, factor_output.T) / replicas
    new_error_query = (total_query - approx_query)[None]
    new_error_output = (total_output - approx_output)[None]
    rows_block = moment_query.shape[0]
    block_query = lax.dynamic_slice_in_dim(approx_query, shard_index * rows_block, rows_block, 0)
    cols_block = moment_output.shape[1]
    block_output = lax.dynamic_slice_in_dim(approx_output, shard_index * cols_block, cols_block, 1)
    new_moment_query = 0.9 * moment_query + block_query
    new_moment_output = 0.9 * moment_output + block_output
    stepped_query = weight_query - 0.01 * new_moment_query
    stepped_output = weight_output - 0.01 * new_moment_output
    local_vector = grad_vector[0].astype(jnp.float32)
    vector_block = moment_vector.shape[0]
    vector_whole = lax.psum(local_vector, "shard")
    vector_part = lax.dynamic_slice_in_dim(
        vector_whole, shard_index * vector_block, vector_block, 0
    )
    vector_mean = vector_part / replicas
    new_moment_vector = 0.9 * moment_vector + vector_mean
    stepped_vector = weight_vector - 0.01 * new_moment_vector
    new_weight_query, new_weight_output, new_weight_vector = (
        lax.all_gather(stepped_query, "shard", axis=0, tiled=True),
        lax.all_gather(stepped_output, "shard", axis=1, tiled=True),
        lax.all_gather(stepped_vector, "shard", axis=0, tiled=True),
    )
    return (
        new_error_query,
        new_error_output,
        new_moment_query,
        new_moment_output,
        new_weight_query,
        new_weight_output,
        new_moment_vector,
        new_weight_vector,
    )


Z, Y, TENSOR = 4, 2, 4
SHARD = Z * Y
RANK = 32
B = 128
VEC_PAD = 512
SLOTS = 40
f32 = jnp.float32


def nn(left, right):
    return lax.dot_general(left, right, (((1,), (0,)), ((), ())), precision=highest, preferred_element_type=f32)


def nt(left, right):
    return lax.dot_general(left, right, (((1,), (1,)), ((), ())), precision=highest, preferred_element_type=f32)


def inverse_lower(gram):
    row = lax.broadcasted_iota(jnp.int32, (RANK, RANK), 0)
    lane = lax.broadcasted_iota(jnp.int32, (RANK, RANK), 1)
    left, right = gram, (row == lane).astype(f32)
    for k in range(0, RANK, 2):
        first = jnp.broadcast_to(left[:, k : k + 1], (RANK, RANK))
        second = jnp.broadcast_to(left[:, k + 1 : k + 2], (RANK, RANK))
        over = 1.0 / first[k : k + 1]
        cross = first[k + 1 : k + 2]
        ratio = cross * over
        under = 1.0 / (second[k + 1 : k + 2] - cross * ratio)

        def reduced(matrix):
            top, low = matrix[k : k + 1], matrix[k + 1 : k + 2]
            low = (low - ratio * matrix[k : k + 1]) * under
            rest = first * (top * over - ratio * low) + second * low
            return matrix - jnp.where(row > k + 1, rest, jnp.where(row == k + 1, ratio * top, 0.0))

        left, right = reduced(left), reduced(right)
    diagonal = jnp.sum(jnp.where(row == lane, left, 0.0), axis=1, keepdims=True)
    return right * lax.rsqrt(diagonal)


def kernel(
    grad_q, error_q, grad_o, error_o, start_q, start_o, weight_q, weight_o, moment_q, moment_o,
    grad_v, moment_v, weight_v,
    keep_tot, keep_wall, keep_pall, keep_fall, keep_q, keep_o, keep_moments, keep_vall, new_moment_v,
    tot, wall, pall, fall, side_q, side_o, moments, vall, gq, eq, go, eo, sq, so, weights, yrecv, zrecv, blk, xq, xo, scat, got, gath, vpart, vrecv,
    send_sem, recv_sem, load_sem, keep_sem,
):
    s, t = lax.axis_index("shard"), lax.axis_index("tensor")
    z, y = s // Y, s % Y
    loads = [pltpu.make_async_copy(src, dst, load_sem.at[i])
             for i, (src, dst) in enumerate((
                 (grad_q, gq), (error_q, eq), (grad_o, go), (error_o, eo), (start_q, sq), (start_o, so),
                 (weight_q, weights.at[0]), (weight_o, weights.at[1]),
                 (moment_q, moments.at[0]), (moment_o, moments.at[1]),
             ))]
    for load in loads:
        load.start()
    barrier = pltpu.get_barrier_semaphore()
    for k in range(1, SHARD):
        pl.semaphore_signal(barrier, inc=1, device_id=((s + k) % SHARD, t), device_id_type=pl.DeviceIdType.MESH)
    for k in range(1, TENSOR):
        pl.semaphore_signal(barrier, inc=1, device_id=(s, (t + k) % TENSOR), device_id_type=pl.DeviceIdType.MESH)

    kept = []

    def keep(src, dst):
        copy = pltpu.make_async_copy(src, dst, keep_sem.at[len(kept)])
        copy.start()
        kept.append(copy)

    used = [0]
    sent = []

    def group(copies, many):
        slot = used[0]
        used[0] += 1
        for src, dst, device in copies:
            pltpu.make_async_remote_copy(
                src_ref=src, dst_ref=dst, send_sem=send_sem.at[slot], recv_sem=recv_sem.at[slot],
                device_id=device, device_id_type=pl.DeviceIdType.MESH).start()
        sent.append((many, slot))
        return lambda: pltpu.make_async_copy(many, many, recv_sem.at[slot]).wait()

    def spread_shard(buf):
        return group([(buf.at[s], buf.at[s], ((s + k) % SHARD, t)) for k in range(1, SHARD)], buf.at[pl.ds(0, SHARD - 1)])

    def spread_tensor(buf):
        return group([(buf.at[t], buf.at[t], (s, (t + k) % TENSOR)) for k in range(1, TENSOR)], buf.at[pl.ds(0, TENSOR - 1)])

    def scatter_shard(src, dst):
        return group([(src.at[(s + k) % SHARD], dst.at[k - 1], ((s + k) % SHARD, t)) for k in range(1, SHARD)], dst)

    for load in loads:
        load.wait()
    for j in range(SHARD):
        tot[j, 0] = gq[j * B : (j + 1) * B, :].astype(f32) + eq[j * B : (j + 1) * B, :]
        tot[j, 1] = go[:, j * B : (j + 1) * B].astype(f32) + eo[:, j * B : (j + 1) * B]
    pl.semaphore_wait(barrier, SHARD - 1 + TENSOR - 1)

    partner = (z * Y + 1 - y, t)
    order = [(z + k) % Z for k in (1, 2, 3, 0)]
    y_waits = [group([(tot.at[c * Y + 1 - y], yrecv.at[c], partner)], yrecv.at[c]) for c in order]
    keep(tot, keep_tot)
    keep(moments, keep_moments)
    wall[s] = weights[...] - 0.01 * (0.9 * moments[...])
    vec = grad_v[...].astype(f32)
    length = moment_v.shape[1]
    vpart[...] = jnp.zeros_like(vpart)
    vall[s] = jnp.zeros((1, VEC_PAD), f32)
    for j in range(SHARD):
        vpart[j, :, 0:length] = vec[:, j * length : (j + 1) * length]
    vector_wait = scatter_shard(vpart, vrecv)
    z_waits = []
    for k, c in enumerate(order[:3]):
        y_waits[k]()
        yrecv[c] = yrecv[c] + tot[c * Y + y]
        z_waits.append(group([(yrecv.at[c], zrecv.at[k], (c * Y + y, t))], zrecv.at[k]))
    y_waits[3]()
    total = yrecv[z] + tot[s]
    w_waits = [group([(wall.at[s], wall.at[s], (((z + k) % Z) * Y + y, t))], wall.at[((z + Z - k) % Z) * Y + y]) for k in (1, 2, 3)]
    w_y_waits = [group([(wall.at[s], wall.at[s], partner)], wall.at[z * Y + 1 - y])]

    def forward(k):
        c = (z + Z - k) % Z
        w_waits[k - 1]()
        w_y_waits.append(group([(wall.at[c * Y + y], wall.at[c * Y + y], partner)], wall.at[c * Y + 1 - y]))

    for k in range(Z - 1):
        z_waits[k]()
        total = total + zrecv[k]
    blk[...] = total

    vector_wait()
    vector_sum = vpart[s]
    for k in range(SHARD - 1):
        vector_sum = vector_sum + vrecv[k]
    moment = 0.9 * moment_v[...] + vector_sum[:, 0:length] / SHARD
    new_moment_v[...] = moment
    vall[s, :, 0:length] = weight_v[...] - 0.01 * moment
    vall_wait = spread_shard(vall)

    factor_q = sq[...]
    factor_o = so[:, pl.ds(pl.multiple_of(s * B, B), B)]
    inverse_q = inverse_o = None
    for turn in range(ROUNDS):
        last = turn == ROUNDS - 1
        a, b = 2 * turn, 2 * turn + 1
        part_o = nt(factor_o, blk[1])
        for j in range(RANK // 8):
            scat[a, j] = part_o[8 * j : 8 * j + 8]
            scat[a, j + RANK // 8] = jnp.zeros((8, B), f32)
        scat_wait = scatter_shard(scat.at[a], got.at[a])
        xq[turn, t] = nt(factor_q, blk[0])
        xq_wait = spread_tensor(xq.at[turn])
        if turn:
            inverse_q, inverse_o = inverse_lower(gram_q), inverse_lower(gram_o)
        xq_wait()
        left_q = xq[turn, 0] + xq[turn, 1] + xq[turn, 2] + xq[turn, 3]
        if turn:
            left_q = nn(inverse_q, left_q)
        right_q = nn(left_q, blk[0])
        square_q = nt(left_q, left_q)
        for j in range(RANK // 8):
            scat[b, j] = right_q[8 * j : 8 * j + 8]
            scat[b, j + RANK // 8] = jnp.zeros((8, B), f32)
            scat[b, j + RANK // 8, :, 0:RANK] = square_q[8 * j : 8 * j + 8]
        q_wait = scatter_shard(scat.at[b], got.at[b])
        scat_wait()
        piece = scat[a, s]
        for k in range(SHARD - 1):
            piece = piece + got[a, k]
        gath[a, s] = piece
        o_wait = spread_shard(gath.at[a])
        if last:
            pall[s] = left_q
            pall_wait = spread_shard(pall)
            forward(2)
        q_wait()
        piece = scat[b, s]
        for k in range(SHARD - 1):
            piece = piece + got[b, k]
        gath[b, s] = piece
        q_wait = spread_shard(gath.at[b])
        o_wait()
        left_o = gath[a, 0 : RANK // 8].reshape(RANK, B)
        if turn:
            left_o = nn(inverse_o, left_o)
        xo[turn, t, 0:RANK] = nn(left_o, blk[1])
        xo[turn, t, RANK : 2 * RANK] = jnp.zeros((RANK, B), f32)
        xo[turn, t, RANK : 2 * RANK, 0:RANK] = nt(left_o, left_o)
        xo_wait = spread_tensor(xo.at[turn])
        forward(3 if last else 1)
        q_wait()
        factor_q = gath[b, 0 : RANK // 8].reshape(RANK, B)
        gram_q = gath[b, RANK // 8 : SHARD].reshape(RANK, B)[:, 0:RANK]
        xo_wait()
        both = xo[turn, 0] + xo[turn, 1] + xo[turn, 2] + xo[turn, 3]
        factor_o, gram_o = both[0:RANK], both[RANK : 2 * RANK, 0:RANK]

    fall[s] = factor_o
    fall_wait = spread_shard(fall)
    inverse_q, inverse_o = inverse_lower(gram_q), inverse_lower(gram_o)
    side_q[...] = nn(inverse_q.T, nn(inverse_q, factor_q)) / SHARD
    side_o[...] = (nn(inverse_o.T, nn(inverse_o, left_o)) / SHARD).T
    keep(side_q, keep_q)
    keep(side_o, keep_o)
    pall_wait()
    keep(pall, keep_pall)
    vall_wait()
    keep(vall, keep_vall)
    fall_wait()
    keep(fall, keep_fall)
    for wait in w_y_waits:
        wait()
    keep(wall, keep_wall)
    for many, slot in sent:
        pltpu.make_async_copy(many, many, send_sem.at[slot]).wait()
    for copy in kept:
        copy.wait()


def finish(
    keep_tot, keep_wall, keep_pall, keep_fall, keep_q, keep_o, keep_moments, keep_vall, moment_v,
    new_error_q, new_error_o, new_moment_q, new_moment_o, new_weight_q, new_weight_o, new_moment_v, new_weight_v,
    tot, wall, pall, fall, side_q, side_o, moments, vall, eq, eo, mq, mo, wq, wo, sem, load_sem,
):
    pairs = (
        (keep_q, side_q), (keep_o, side_o), (keep_pall, pall), (keep_fall, fall), (keep_moments, moments),
        (keep_tot, tot), (keep_wall, wall), (keep_vall, vall),
    )
    loads = [pltpu.make_async_copy(src, dst, load_sem.at[i]) for i, (src, dst) in enumerate(pairs)]
    for load in loads:
        load.start()
    s = lax.axis_index("shard")
    out = []

    def leave(src, dst):
        copy = pltpu.make_async_copy(src, dst, sem.at[len(out)])
        copy.start()
        out.append(copy)

    for load in loads:
        load.wait()
    mq[...] = 0.9 * moments[0] + nn(pall[s].T, side_q[...])
    mo[...] = 0.9 * moments[1] + nn(side_o[...], fall[s])
    leave(mq, new_moment_q)
    leave(mo, new_moment_o)
    for j in range(SHARD):
        rows = pl.ds(j * B, B)
        approx = nn(pall[j].T, side_q[...])
        eq[rows, :] = tot[j, 0] - approx
        wq[rows, :] = wall[j, 0] - 0.01 * approx
        approx = nn(side_o[...], fall[j])
        eo[:, rows] = tot[j, 1] - approx
        wo[:, rows] = wall[j, 1] - 0.01 * approx
        if j % 2:
            pair = pl.ds((j - 1) * B, 2 * B)
            leave(eq.at[pair, :], new_error_q.at[pair, :])
            leave(wq.at[pair, :], new_weight_q.at[pair, :])
            leave(eo.at[:, pair], new_error_o.at[:, pair])
            leave(wo.at[:, pair], new_weight_o.at[:, pair])
    length = moment_v.shape[1]
    new_moment_v[...] = moment_v[...]
    for j in range(SHARD):
        new_weight_v[:, j * length : (j + 1) * length] = vall[j, :, 0:length]
    for copy in out:
        copy.wait()


def fast_local(
    grad_query, error_query, grad_output, error_output, start_query, start_output, weight_query, weight_output,
    moment_query, moment_output, grad_vector, moment_vector, weight_vector,
):
    length = moment_vector.shape[0]
    vmem = pl.BlockSpec(memory_space=pltpu.VMEM)
    hbm = pl.BlockSpec(memory_space=pltpu.HBM)
    shape = lambda *dims: jax.ShapeDtypeStruct(dims, f32)
    scratch = lambda *dims: pltpu.VMEM(dims, f32)
    kept = pl.pallas_call(
        kernel,
        out_shape=(
            shape(SHARD, 2, B, B), shape(SHARD, 2, B, B), shape(SHARD, RANK, B), shape(SHARD, RANK, B),
            shape(RANK, B), shape(B, RANK), shape(2, B, B), shape(SHARD, 1, VEC_PAD), shape(1, length),
        ),
        in_specs=[hbm] * 10 + [vmem] * 3,
        out_specs=(hbm,) * 8 + (vmem,),
        scratch_shapes=[
            scratch(SHARD, 2, B, B), scratch(SHARD, 2, B, B), scratch(SHARD, RANK, B), scratch(SHARD, RANK, B),
            scratch(RANK, B), scratch(B, RANK), scratch(2, B, B), scratch(SHARD, 1, VEC_PAD),
            pltpu.VMEM((SHARD * B, B), grad_query.dtype), scratch(SHARD * B, B),
            pltpu.VMEM((B, SHARD * B), grad_output.dtype), scratch(B, SHARD * B),
            scratch(RANK, B), scratch(RANK, SHARD * B), scratch(2, B, B),
            scratch(Z, 2, B, B), scratch(Z - 1, 2, B, B), scratch(2, B, B),
            scratch(ROUNDS, TENSOR, RANK, B), scratch(ROUNDS, TENSOR, 2 * RANK, B),
            scratch(2 * ROUNDS, SHARD, 8, B), scratch(2 * ROUNDS, SHARD - 1, 8, B), scratch(2 * ROUNDS, SHARD, 8, B),
            scratch(SHARD, 1, VEC_PAD), scratch(SHARD - 1, 1, VEC_PAD),
            pltpu.SemaphoreType.DMA((SLOTS,)), pltpu.SemaphoreType.DMA((SLOTS,)), pltpu.SemaphoreType.DMA((10,)), pltpu.SemaphoreType.DMA((8,)),
        ],
        compiler_params=pltpu.CompilerParams(collective_id=0, has_side_effects=True, vmem_limit_bytes=60 * 2**20),
        cost_estimate=pl.CostEstimate(flops=2**30, bytes_accessed=5 * 2**20, transcendentals=0),
    )(
        grad_query[0], error_query[0], grad_output[0], error_output[0], start_query.T, start_output.T,
        weight_query, weight_output, moment_query, moment_output,
        grad_vector, moment_vector[None], weight_vector[None],
    )
    eq, eo, mq, mo, wq, wo, mv, wv = pl.pallas_call(
        finish,
        out_shape=(
            shape(SHARD * B, B), shape(B, SHARD * B), shape(B, B), shape(B, B),
            shape(SHARD * B, B), shape(B, SHARD * B), shape(1, length), shape(1, SHARD * length),
        ),
        in_specs=[hbm] * 8 + [vmem],
        out_specs=(hbm,) * 6 + (vmem,) * 2,
        scratch_shapes=[
            scratch(SHARD, 2, B, B), scratch(SHARD, 2, B, B), scratch(SHARD, RANK, B), scratch(SHARD, RANK, B),
            scratch(RANK, B), scratch(B, RANK), scratch(2, B, B), scratch(SHARD, 1, VEC_PAD),
            scratch(SHARD * B, B), scratch(B, SHARD * B), scratch(B, B), scratch(B, B),
            scratch(SHARD * B, B), scratch(B, SHARD * B), pltpu.SemaphoreType.DMA((2 + 2 * SHARD,)),
            pltpu.SemaphoreType.DMA((8,)),
        ],
        compiler_params=pltpu.CompilerParams(vmem_limit_bytes=60 * 2**20),
        cost_estimate=pl.CostEstimate(flops=2**26, bytes_accessed=5 * 2**20, transcendentals=0),
    )(*kept)
    return eq[None], eo[None], mq, mo, wq, wo, mv[0], wv[0]


def solution(mesh):
    in_specs = (
        P("shard", None, "tensor"),
        P("shard", None, "tensor"),
        P("shard", "tensor", None),
        P("shard", "tensor", None),
        P("tensor", None),
        P(),
        P("shard", "tensor"),
        P("tensor", "shard"),
        P("shard", "tensor"),
        P("tensor", "shard"),
        P("shard", None),
        P("shard"),
        P("shard"),
    )
    out_specs = (
        P("shard", None, "tensor"),
        P("shard", "tensor", None),
        P("shard", "tensor"),
        P("tensor", "shard"),
        P(None, "tensor"),
        P("tensor", None),
        P("shard"),
        P(),
    )
    body = fast_local if (mesh.shape["shard"], mesh.shape["tensor"]) == (Z * Y, TENSOR) else local
    return jax.shard_map(body, mesh=mesh, in_specs=in_specs, out_specs=out_specs, check_vma=False)
```

```python
import jax
import jax.numpy as jnp
from jax import lax
from jax.experimental import pallas as pl
from jax.experimental.pallas import tpu as pltpu
from jax.sharding import PartitionSpec as P

ROUNDS = 2


highest = lax.Precision.HIGHEST


def product(left, right):
    return jnp.dot(left, right, precision=highest, preferred_element_type=jnp.float32)


def product_inner(left, right):
    return lax.dot_general(
        left, right, (((0,), (0,)), ((), ())), precision=highest, preferred_element_type=jnp.float32
    )


def solve_rows(gram, factor):
    lower = jnp.linalg.cholesky(gram)
    return jax.scipy.linalg.solve_triangular(lower, factor.T, lower=True).T


def orthonormal(factor):
    return solve_rows(product_inner(factor, factor), factor)


def orthonormal_rows(factor):
    gram = lax.psum(product_inner(factor, factor), "tensor")
    return solve_rows(gram, factor)


def local(
    grad_query,
    error_query,
    grad_output,
    error_output,
    start_query,
    start_output,
    weight_query,
    weight_output,
    moment_query,
    moment_output,
    grad_vector,
    moment_vector,
    weight_vector,
):
    replicas = lax.axis_size("shard")
    shard_index = lax.axis_index("shard")
    total_query = grad_query[0].astype(jnp.float32) + error_query[0]
    total_output = grad_output[0].astype(jnp.float32) + error_output[0]
    factor_query = start_query
    factor_output = start_output
    for turn in range(ROUNDS):
        part_query = product(total_query, factor_query)
        part_output = product(total_output, factor_output)
        sum_query = lax.psum(part_query, ("shard", "tensor"))
        sum_output = lax.psum(part_output, "shard")
        left_query = orthonormal(sum_query)
        left_output = orthonormal_rows(sum_output)
        right_query_part = product_inner(total_query, left_query)
        right_output_part = product_inner(total_output, left_output)
        factor_query = lax.psum(right_query_part, "shard")
        factor_output = lax.psum(right_output_part, ("shard", "tensor"))
    approx_query = product(left_query, factor_query.T) / replicas
    approx_output = product(left_output, factor_output.T) / replicas
    new_error_query = (total_query - approx_query)[None]
    new_error_output = (total_output - approx_output)[None]
    rows_block = moment_query.shape[0]
    block_query = lax.dynamic_slice_in_dim(approx_query, shard_index * rows_block, rows_block, 0)
    cols_block = moment_output.shape[1]
    block_output = lax.dynamic_slice_in_dim(approx_output, shard_index * cols_block, cols_block, 1)
    new_moment_query = 0.9 * moment_query + block_query
    new_moment_output = 0.9 * moment_output + block_output
    stepped_query = weight_query - 0.01 * new_moment_query
    stepped_output = weight_output - 0.01 * new_moment_output
    local_vector = grad_vector[0].astype(jnp.float32)
    vector_block = moment_vector.shape[0]
    vector_whole = lax.psum(local_vector, "shard")
    vector_part = lax.dynamic_slice_in_dim(
        vector_whole, shard_index * vector_block, vector_block, 0
    )
    vector_mean = vector_part / replicas
    new_moment_vector = 0.9 * moment_vector + vector_mean
    stepped_vector = weight_vector - 0.01 * new_moment_vector
    new_weight_query, new_weight_output, new_weight_vector = (
        lax.all_gather(stepped_query, "shard", axis=0, tiled=True),
        lax.all_gather(stepped_output, "shard", axis=1, tiled=True),
        lax.all_gather(stepped_vector, "shard", axis=0, tiled=True),
    )
    return (
        new_error_query,
        new_error_output,
        new_moment_query,
        new_moment_output,
        new_weight_query,
        new_weight_output,
        new_moment_vector,
        new_weight_vector,
    )


Z, Y, TENSOR = 4, 2, 4
SHARD = Z * Y
RANK = 32
B = 128
VEC_PAD = 512
SLOTS = 40
f32 = jnp.float32


def nn(left, right):
    return lax.dot_general(left, right, (((1,), (0,)), ((), ())), precision=highest, preferred_element_type=f32)


def nt(left, right):
    return lax.dot_general(left, right, (((1,), (1,)), ((), ())), precision=highest, preferred_element_type=f32)


def inverse_lower(gram):
    row = lax.broadcasted_iota(jnp.int32, (RANK, RANK), 0)
    lane = lax.broadcasted_iota(jnp.int32, (RANK, RANK), 1)
    left, right = gram, (row == lane).astype(f32)
    for k in range(0, RANK, 2):
        first = jnp.broadcast_to(left[:, k : k + 1], (RANK, RANK))
        second = jnp.broadcast_to(left[:, k + 1 : k + 2], (RANK, RANK))
        over = 1.0 / first[k : k + 1]
        cross = first[k + 1 : k + 2]
        ratio = cross * over
        under = 1.0 / (second[k + 1 : k + 2] - cross * ratio)

        def reduced(matrix):
            top, low = matrix[k : k + 1], matrix[k + 1 : k + 2]
            low = (low - ratio * matrix[k : k + 1]) * under
            rest = first * (top * over - ratio * low) + second * low
            return matrix - jnp.where(row > k + 1, rest, jnp.where(row == k + 1, ratio * top, 0.0))

        left, right = reduced(left), reduced(right)
    diagonal = jnp.sum(jnp.where(row == lane, left, 0.0), axis=1, keepdims=True)
    return right * lax.rsqrt(diagonal)


def kernel(
    grad_q, error_q, grad_o, error_o, start_q, start_o, weight_q, weight_o, moment_q, moment_o,
    grad_v, moment_v, weight_v,
    keep_tot, keep_wall, keep_pall, keep_fall, keep_q, keep_o, keep_moments, keep_vall, new_moment_v,
    tot, wall, pall, fall, side_q, side_o, moments, vall, gq, eq, go, eo, sq, so, weights, yrecv, zrecv, blk, xq, xo, scat, got, gath, vpart, vrecv,
    send_sem, recv_sem, load_sem, keep_sem,
):
    s, t = lax.axis_index("shard"), lax.axis_index("tensor")
    z, y = s // Y, s % Y
    loads = [pltpu.make_async_copy(src, dst, load_sem.at[i])
             for i, (src, dst) in enumerate((
                 (grad_q, gq), (error_q, eq), (grad_o, go), (error_o, eo), (start_q, sq), (start_o, so),
                 (weight_q, weights.at[0]), (weight_o, weights.at[1]),
                 (moment_q, moments.at[0]), (moment_o, moments.at[1]),
             ))]
    for load in loads:
        load.start()
    barrier = pltpu.get_barrier_semaphore()
    for k in range(1, SHARD):
        pl.semaphore_signal(barrier, inc=1, device_id=((s + k) % SHARD, t), device_id_type=pl.DeviceIdType.MESH)
    for k in range(1, TENSOR):
        pl.semaphore_signal(barrier, inc=1, device_id=(s, (t + k) % TENSOR), device_id_type=pl.DeviceIdType.MESH)

    kept = []

    def keep(src, dst):
        copy = pltpu.make_async_copy(src, dst, keep_sem.at[len(kept)])
        copy.start()
        kept.append(copy)

    used = [0]
    sent = []

    def group(copies, many):
        slot = used[0]
        used[0] += 1
        for src, dst, device in copies:
            pltpu.make_async_remote_copy(
                src_ref=src, dst_ref=dst, send_sem=send_sem.at[slot], recv_sem=recv_sem.at[slot],
                device_id=device, device_id_type=pl.DeviceIdType.MESH).start()
        sent.append((many, slot))
        return lambda: pltpu.make_async_copy(many, many, recv_sem.at[slot]).wait()

    def spread_shard(buf):
        return group([(buf.at[s], buf.at[s], ((s + k) % SHARD, t)) for k in range(1, SHARD)], buf.at[pl.ds(0, SHARD - 1)])

    def spread_tensor(buf):
        return group([(buf.at[t], buf.at[t], (s, (t + k) % TENSOR)) for k in range(1, TENSOR)], buf.at[pl.ds(0, TENSOR - 1)])

    def scatter_shard(src, dst):
        return group([(src.at[(s + k) % SHARD], dst.at[k - 1], ((s + k) % SHARD, t)) for k in range(1, SHARD)], dst)

    for load in loads:
        load.wait()
    for j in range(SHARD):
        tot[j, 0] = gq[j * B : (j + 1) * B, :].astype(f32) + eq[j * B : (j + 1) * B, :]
        tot[j, 1] = go[:, j * B : (j + 1) * B].astype(f32) + eo[:, j * B : (j + 1) * B]
    pl.semaphore_wait(barrier, SHARD - 1 + TENSOR - 1)

    partner = (z * Y + 1 - y, t)
    order = [(z + k) % Z for k in (1, 2, 3, 0)]
    y_waits = [group([(tot.at[c * Y + 1 - y], yrecv.at[c], partner)], yrecv.at[c]) for c in order]
    keep(tot, keep_tot)
    keep(moments, keep_moments)
    wall[s] = weights[...] - 0.01 * (0.9 * moments[...])
    w_waits, w_y_waits = {}, []

    def along_z(k):
        w_waits[k] = group([(wall.at[s], wall.at[s], (((z + k) % Z) * Y + y, t))], wall.at[((z + Z - k) % Z) * Y + y])

    def own_to_partner():
        w_y_waits.append(group([(wall.at[s], wall.at[s], partner)], wall.at[z * Y + 1 - y]))

    def forward(k):
        c = (z + Z - k) % Z
        w_waits[k]()
        w_y_waits.append(group([(wall.at[c * Y + y], wall.at[c * Y + y], partner)], wall.at[c * Y + 1 - y]))

    along_z(1)
    along_z(3)
    vec = grad_v[...].astype(f32)
    length = moment_v.shape[1]
    vpart[...] = jnp.zeros_like(vpart)
    vall[s] = jnp.zeros((1, VEC_PAD), f32)
    for j in range(SHARD):
        vpart[j, :, 0:length] = vec[:, j * length : (j + 1) * length]
    vector_wait = scatter_shard(vpart, vrecv)
    z_waits = []
    for k, c in enumerate(order[:3]):
        y_waits[k]()
        yrecv[c] = yrecv[c] + tot[c * Y + y]
        z_waits.append(group([(yrecv.at[c], zrecv.at[k], (c * Y + y, t))], zrecv.at[k]))
    y_waits[3]()
    total = yrecv[z] + tot[s]
    own_to_partner()
    forward(1)
    forward(3)

    for k in range(Z - 1):
        z_waits[k]()
        total = total + zrecv[k]
    blk[...] = total

    vector_wait()
    vector_sum = vpart[s]
    for k in range(SHARD - 1):
        vector_sum = vector_sum + vrecv[k]
    moment = 0.9 * moment_v[...] + vector_sum[:, 0:length] / SHARD
    new_moment_v[...] = moment
    vall[s, :, 0:length] = weight_v[...] - 0.01 * moment
    vall_wait = spread_shard(vall)

    factor_q = sq[...]
    factor_o = so[:, pl.ds(pl.multiple_of(s * B, B), B)]
    inverse_q = inverse_o = None
    for turn in range(ROUNDS):
        last = turn == ROUNDS - 1
        a, b = 2 * turn, 2 * turn + 1
        part_o = nt(factor_o, blk[1])
        for j in range(RANK // 8):
            scat[a, j] = part_o[8 * j : 8 * j + 8]
            scat[a, j + RANK // 8] = jnp.zeros((8, B), f32)
        scat_wait = scatter_shard(scat.at[a], got.at[a])
        xq[turn, t] = nt(factor_q, blk[0])
        xq_wait = spread_tensor(xq.at[turn])
        if not last:
            along_z(2)
        if turn:
            inverse_q, inverse_o = inverse_lower(gram_q), inverse_lower(gram_o)
        xq_wait()
        left_q = xq[turn, 0] + xq[turn, 1] + xq[turn, 2] + xq[turn, 3]
        if turn:
            left_q = nn(inverse_q, left_q)
        right_q = nn(left_q, blk[0])
        square_q = nt(left_q, left_q)
        for j in range(RANK // 8):
            scat[b, j] = right_q[8 * j : 8 * j + 8]
            scat[b, j + RANK // 8] = jnp.zeros((8, B), f32)
            scat[b, j + RANK // 8, :, 0:RANK] = square_q[8 * j : 8 * j + 8]
        q_wait = scatter_shard(scat.at[b], got.at[b])
        scat_wait()
        piece = scat[a, s]
        for k in range(SHARD - 1):
            piece = piece + got[a, k]
        gath[a, s] = piece
        o_wait = spread_shard(gath.at[a])
        if last:
            pall[s] = left_q
            pall_wait = spread_shard(pall)
        q_wait()
        piece = scat[b, s]
        for k in range(SHARD - 1):
            piece = piece + got[b, k]
        gath[b, s] = piece
        q_wait = spread_shard(gath.at[b])
        o_wait()
        left_o = gath[a, 0 : RANK // 8].reshape(RANK, B)
        if turn:
            left_o = nn(inverse_o, left_o)
        xo[turn, t, 0:RANK] = nn(left_o, blk[1])
        xo[turn, t, RANK : 2 * RANK] = jnp.zeros((RANK, B), f32)
        xo[turn, t, RANK : 2 * RANK, 0:RANK] = nt(left_o, left_o)
        xo_wait = spread_tensor(xo.at[turn])
        if not last:
            forward(2)
        q_wait()
        factor_q = gath[b, 0 : RANK // 8].reshape(RANK, B)
        gram_q = gath[b, RANK // 8 : SHARD].reshape(RANK, B)[:, 0:RANK]
        xo_wait()
        both = xo[turn, 0] + xo[turn, 1] + xo[turn, 2] + xo[turn, 3]
        factor_o, gram_o = both[0:RANK], both[RANK : 2 * RANK, 0:RANK]

    fall[s] = factor_o
    fall_wait = spread_shard(fall)
    inverse_q, inverse_o = inverse_lower(gram_q), inverse_lower(gram_o)
    side_q[...] = nn(inverse_q.T, nn(inverse_q, factor_q)) / SHARD
    side_o[...] = (nn(inverse_o.T, nn(inverse_o, left_o)) / SHARD).T
    keep(side_q, keep_q)
    keep(side_o, keep_o)
    pall_wait()
    keep(pall, keep_pall)
    vall_wait()
    keep(vall, keep_vall)
    fall_wait()
    keep(fall, keep_fall)
    for wait in w_y_waits:
        wait()
    keep(wall, keep_wall)
    for many, slot in sent:
        pltpu.make_async_copy(many, many, send_sem.at[slot]).wait()
    for copy in kept:
        copy.wait()


def finish(
    keep_tot, keep_wall, keep_pall, keep_fall, keep_q, keep_o, keep_moments, keep_vall, moment_v,
    new_error_q, new_error_o, new_moment_q, new_moment_o, new_weight_q, new_weight_o, new_moment_v, new_weight_v,
    tot, wall, pall, fall, side_q, side_o, moments, vall, eq, eo, mq, mo, wq, wo, sem, load_sem,
):
    pairs = (
        (keep_q, side_q), (keep_o, side_o), (keep_pall, pall), (keep_fall, fall), (keep_moments, moments),
        (keep_tot, tot), (keep_wall, wall), (keep_vall, vall),
    )
    loads = [pltpu.make_async_copy(src, dst, load_sem.at[i]) for i, (src, dst) in enumerate(pairs)]
    for load in loads:
        load.start()
    s = lax.axis_index("shard")
    out = []

    def leave(src, dst):
        copy = pltpu.make_async_copy(src, dst, sem.at[len(out)])
        copy.start()
        out.append(copy)

    for load in loads[:5]:
        load.wait()
    mq[...] = 0.9 * moments[0] + nn(pall[s].T, side_q[...])
    mo[...] = 0.9 * moments[1] + nn(side_o[...], fall[s])
    leave(mq, new_moment_q)
    leave(mo, new_moment_o)
    for load in loads[5:]:
        load.wait()
    for j in range(SHARD):
        rows = pl.ds(j * B, B)
        approx = nn(pall[j].T, side_q[...])
        eq[rows, :] = tot[j, 0] - approx
        wq[rows, :] = wall[j, 0] - 0.01 * approx
        approx = nn(side_o[...], fall[j])
        eo[:, rows] = tot[j, 1] - approx
        wo[:, rows] = wall[j, 1] - 0.01 * approx
        if j % 2:
            pair = pl.ds((j - 1) * B, 2 * B)
            leave(eq.at[pair, :], new_error_q.at[pair, :])
            leave(wq.at[pair, :], new_weight_q.at[pair, :])
            leave(eo.at[:, pair], new_error_o.at[:, pair])
            leave(wo.at[:, pair], new_weight_o.at[:, pair])
    length = moment_v.shape[1]
    new_moment_v[...] = moment_v[...]
    for j in range(SHARD):
        new_weight_v[:, j * length : (j + 1) * length] = vall[j, :, 0:length]
    for copy in out:
        copy.wait()


def fast_local(
    grad_query, error_query, grad_output, error_output, start_query, start_output, weight_query, weight_output,
    moment_query, moment_output, grad_vector, moment_vector, weight_vector,
):
    length = moment_vector.shape[0]
    vmem = pl.BlockSpec(memory_space=pltpu.VMEM)
    hbm = pl.BlockSpec(memory_space=pltpu.HBM)
    shape = lambda *dims: jax.ShapeDtypeStruct(dims, f32)
    scratch = lambda *dims: pltpu.VMEM(dims, f32)
    kept = pl.pallas_call(
        kernel,
        out_shape=(
            shape(SHARD, 2, B, B), shape(SHARD, 2, B, B), shape(SHARD, RANK, B), shape(SHARD, RANK, B),
            shape(RANK, B), shape(B, RANK), shape(2, B, B), shape(SHARD, 1, VEC_PAD), shape(1, length),
        ),
        in_specs=[hbm] * 10 + [vmem] * 3,
        out_specs=(hbm,) * 8 + (vmem,),
        scratch_shapes=[
            scratch(SHARD, 2, B, B), scratch(SHARD, 2, B, B), scratch(SHARD, RANK, B), scratch(SHARD, RANK, B),
            scratch(RANK, B), scratch(B, RANK), scratch(2, B, B), scratch(SHARD, 1, VEC_PAD),
            pltpu.VMEM((SHARD * B, B), grad_query.dtype), scratch(SHARD * B, B),
            pltpu.VMEM((B, SHARD * B), grad_output.dtype), scratch(B, SHARD * B),
            scratch(RANK, B), scratch(RANK, SHARD * B), scratch(2, B, B),
            scratch(Z, 2, B, B), scratch(Z - 1, 2, B, B), scratch(2, B, B),
            scratch(ROUNDS, TENSOR, RANK, B), scratch(ROUNDS, TENSOR, 2 * RANK, B),
            scratch(2 * ROUNDS, SHARD, 8, B), scratch(2 * ROUNDS, SHARD - 1, 8, B), scratch(2 * ROUNDS, SHARD, 8, B),
            scratch(SHARD, 1, VEC_PAD), scratch(SHARD - 1, 1, VEC_PAD),
            pltpu.SemaphoreType.DMA((SLOTS,)), pltpu.SemaphoreType.DMA((SLOTS,)), pltpu.SemaphoreType.DMA((10,)), pltpu.SemaphoreType.DMA((8,)),
        ],
        compiler_params=pltpu.CompilerParams(collective_id=0, has_side_effects=True, vmem_limit_bytes=60 * 2**20),
        cost_estimate=pl.CostEstimate(flops=2**30, bytes_accessed=5 * 2**20, transcendentals=0),
    )(
        grad_query[0], error_query[0], grad_output[0], error_output[0], start_query.T, start_output.T,
        weight_query, weight_output, moment_query, moment_output,
        grad_vector, moment_vector[None], weight_vector[None],
    )
    eq, eo, mq, mo, wq, wo, mv, wv = pl.pallas_call(
        finish,
        out_shape=(
            shape(SHARD * B, B), shape(B, SHARD * B), shape(B, B), shape(B, B),
            shape(SHARD * B, B), shape(B, SHARD * B), shape(1, length), shape(1, SHARD * length),
        ),
        in_specs=[hbm] * 8 + [vmem],
        out_specs=(hbm,) * 6 + (vmem,) * 2,
        scratch_shapes=[
            scratch(SHARD, 2, B, B), scratch(SHARD, 2, B, B), scratch(SHARD, RANK, B), scratch(SHARD, RANK, B),
            scratch(RANK, B), scratch(B, RANK), scratch(2, B, B), scratch(SHARD, 1, VEC_PAD),
            scratch(SHARD * B, B), scratch(B, SHARD * B), scratch(B, B), scratch(B, B),
            scratch(SHARD * B, B), scratch(B, SHARD * B), pltpu.SemaphoreType.DMA((2 + 2 * SHARD,)),
            pltpu.SemaphoreType.DMA((8,)),
        ],
        compiler_params=pltpu.CompilerParams(vmem_limit_bytes=60 * 2**20),
        cost_estimate=pl.CostEstimate(flops=2**26, bytes_accessed=5 * 2**20, transcendentals=0),
    )(*kept)
    return eq[None], eo[None], mq, mo, wq, wo, mv.reshape(-1), wv.reshape(-1)


def solution(mesh):
    in_specs = (
        P("shard", None, "tensor"),
        P("shard", None, "tensor"),
        P("shard", "tensor", None),
        P("shard", "tensor", None),
        P("tensor", None),
        P(),
        P("shard", "tensor"),
        P("tensor", "shard"),
        P("shard", "tensor"),
        P("tensor", "shard"),
        P("shard", None),
        P("shard"),
        P("shard"),
    )
    out_specs = (
        P("shard", None, "tensor"),
        P("shard", "tensor", None),
        P("shard", "tensor"),
        P("tensor", "shard"),
        P(None, "tensor"),
        P("tensor", None),
        P("shard"),
        P(),
    )
    body = fast_local if (mesh.shape["shard"], mesh.shape["tensor"]) == (Z * Y, TENSOR) else local
    return jax.shard_map(body, mesh=mesh, in_specs=in_specs, out_specs=out_specs, check_vma=False)
```

```python
import jax
import jax.numpy as jnp
from jax import lax
from jax.experimental import pallas as pl
from jax.experimental.pallas import tpu as pltpu
from jax.sharding import PartitionSpec as P

ROUNDS = 2


highest = lax.Precision.HIGHEST


def product(left, right):
    return jnp.dot(left, right, precision=highest, preferred_element_type=jnp.float32)


def product_inner(left, right):
    return lax.dot_general(
        left, right, (((0,), (0,)), ((), ())), precision=highest, preferred_element_type=jnp.float32
    )


def solve_rows(gram, factor):
    lower = jnp.linalg.cholesky(gram)
    return jax.scipy.linalg.solve_triangular(lower, factor.T, lower=True).T


def orthonormal(factor):
    return solve_rows(product_inner(factor, factor), factor)


def orthonormal_rows(factor):
    gram = lax.psum(product_inner(factor, factor), "tensor")
    return solve_rows(gram, factor)


def local(
    grad_query,
    error_query,
    grad_output,
    error_output,
    start_query,
    start_output,
    weight_query,
    weight_output,
    moment_query,
    moment_output,
    grad_vector,
    moment_vector,
    weight_vector,
):
    replicas = lax.axis_size("shard")
    shard_index = lax.axis_index("shard")
    total_query = grad_query[0].astype(jnp.float32) + error_query[0]
    total_output = grad_output[0].astype(jnp.float32) + error_output[0]
    factor_query = start_query
    factor_output = start_output
    for turn in range(ROUNDS):
        part_query = product(total_query, factor_query)
        part_output = product(total_output, factor_output)
        sum_query = lax.psum(part_query, ("shard", "tensor"))
        sum_output = lax.psum(part_output, "shard")
        left_query = orthonormal(sum_query)
        left_output = orthonormal_rows(sum_output)
        right_query_part = product_inner(total_query, left_query)
        right_output_part = product_inner(total_output, left_output)
        factor_query = lax.psum(right_query_part, "shard")
        factor_output = lax.psum(right_output_part, ("shard", "tensor"))
    approx_query = product(left_query, factor_query.T) / replicas
    approx_output = product(left_output, factor_output.T) / replicas
    new_error_query = (total_query - approx_query)[None]
    new_error_output = (total_output - approx_output)[None]
    rows_block = moment_query.shape[0]
    block_query = lax.dynamic_slice_in_dim(approx_query, shard_index * rows_block, rows_block, 0)
    cols_block = moment_output.shape[1]
    block_output = lax.dynamic_slice_in_dim(approx_output, shard_index * cols_block, cols_block, 1)
    new_moment_query = 0.9 * moment_query + block_query
    new_moment_output = 0.9 * moment_output + block_output
    stepped_query = weight_query - 0.01 * new_moment_query
    stepped_output = weight_output - 0.01 * new_moment_output
    local_vector = grad_vector[0].astype(jnp.float32)
    vector_block = moment_vector.shape[0]
    vector_whole = lax.psum(local_vector, "shard")
    vector_part = lax.dynamic_slice_in_dim(
        vector_whole, shard_index * vector_block, vector_block, 0
    )
    vector_mean = vector_part / replicas
    new_moment_vector = 0.9 * moment_vector + vector_mean
    stepped_vector = weight_vector - 0.01 * new_moment_vector
    new_weight_query, new_weight_output, new_weight_vector = (
        lax.all_gather(stepped_query, "shard", axis=0, tiled=True),
        lax.all_gather(stepped_output, "shard", axis=1, tiled=True),
        lax.all_gather(stepped_vector, "shard", axis=0, tiled=True),
    )
    return (
        new_error_query,
        new_error_output,
        new_moment_query,
        new_moment_output,
        new_weight_query,
        new_weight_output,
        new_moment_vector,
        new_weight_vector,
    )


Z, Y, TENSOR = 4, 2, 4
SHARD = Z * Y
RANK = 32
B = 128
VEC_PAD = 512
SLOTS = 64
f32 = jnp.float32


def nn(left, right):
    return lax.dot_general(left, right, (((1,), (0,)), ((), ())), precision=highest, preferred_element_type=f32)


def nt(left, right):
    return lax.dot_general(left, right, (((1,), (1,)), ((), ())), precision=highest, preferred_element_type=f32)


def inverse_lower(gram):
    row = lax.broadcasted_iota(jnp.int32, (RANK, RANK), 0)
    lane = lax.broadcasted_iota(jnp.int32, (RANK, RANK), 1)
    left, right = gram, (row == lane).astype(f32)
    for k in range(0, RANK, 2):
        first = jnp.broadcast_to(left[:, k : k + 1], (RANK, RANK))
        second = jnp.broadcast_to(left[:, k + 1 : k + 2], (RANK, RANK))
        over = 1.0 / first[k : k + 1]
        cross = first[k + 1 : k + 2]
        ratio = cross * over
        under = 1.0 / (second[k + 1 : k + 2] - cross * ratio)

        def reduced(matrix):
            top, low = matrix[k : k + 1], matrix[k + 1 : k + 2]
            low = (low - ratio * matrix[k : k + 1]) * under
            rest = first * (top * over - ratio * low) + second * low
            return matrix - jnp.where(row > k + 1, rest, jnp.where(row == k + 1, ratio * top, 0.0))

        left, right = reduced(left), reduced(right)
    diagonal = jnp.sum(jnp.where(row == lane, left, 0.0), axis=1, keepdims=True)
    return right * lax.rsqrt(diagonal)


def kernel(
    grad_q, error_q, grad_o, error_o, start_q, start_o, weight_q, weight_o, moment_q, moment_o,
    grad_v, moment_v, weight_v,
    keep_tot, keep_wall, keep_pall, keep_fall, keep_q, keep_o, keep_moments, keep_vall, new_moment_v,
    tot, wall, pall, fall, side_q, side_o, moments, vall, gq, eq, go, eo, sq, so, weights, yrecv, zrecv, blk, xq, xo, scat, got, gath, vpart, vrecv,
    send_sem, recv_sem, load_sem, keep_sem,
):
    s, t = lax.axis_index("shard"), lax.axis_index("tensor")
    z, y = s // Y, s % Y
    loads = [pltpu.make_async_copy(src, dst, load_sem.at[i])
             for i, (src, dst) in enumerate((
                 (grad_q, gq), (error_q, eq), (grad_o, go), (error_o, eo), (start_q, sq), (start_o, so),
                 (weight_q, weights.at[0]), (weight_o, weights.at[1]),
                 (moment_q, moments.at[0]), (moment_o, moments.at[1]),
             ))]
    for load in loads:
        load.start()
    barrier = pltpu.get_barrier_semaphore()
    for k in range(1, SHARD):
        pl.semaphore_signal(barrier, inc=1, device_id=((s + k) % SHARD, t), device_id_type=pl.DeviceIdType.MESH)
    for k in range(1, TENSOR):
        pl.semaphore_signal(barrier, inc=1, device_id=(s, (t + k) % TENSOR), device_id_type=pl.DeviceIdType.MESH)

    kept = []

    def keep(src, dst):
        copy = pltpu.make_async_copy(src, dst, keep_sem.at[len(kept)])
        copy.start()
        kept.append(copy)

    used = [0]
    sent = []

    def group(copies, many):
        slot = used[0]
        used[0] += 1
        for src, dst, device in copies:
            pltpu.make_async_remote_copy(
                src_ref=src, dst_ref=dst, send_sem=send_sem.at[slot], recv_sem=recv_sem.at[slot],
                device_id=device, device_id_type=pl.DeviceIdType.MESH).start()
        sent.append((many, slot))
        return lambda: pltpu.make_async_copy(many, many, recv_sem.at[slot]).wait()

    def spread_shard(buf):
        return group([(buf.at[s], buf.at[s], ((s + k) % SHARD, t)) for k in range(1, SHARD)], buf.at[pl.ds(0, SHARD - 1)])

    def spread_tensor(buf):
        return group([(buf.at[t], buf.at[t], (s, (t + k) % TENSOR)) for k in range(1, TENSOR)], buf.at[pl.ds(0, TENSOR - 1)])

    def scatter_shard(src, dst):
        return group([(src.at[(s + k) % SHARD], dst.at[k - 1], ((s + k) % SHARD, t)) for k in range(1, SHARD)], dst)

    for load in loads:
        load.wait()
    for j in range(SHARD):
        tot[j, 0] = gq[j * B : (j + 1) * B, :].astype(f32) + eq[j * B : (j + 1) * B, :]
        tot[j, 1] = go[:, j * B : (j + 1) * B].astype(f32) + eo[:, j * B : (j + 1) * B]
    pl.semaphore_wait(barrier, SHARD - 1 + TENSOR - 1)

    partner = (z * Y + 1 - y, t)
    order = [(z + k) % Z for k in (1, 2, 3, 0)]

    def along_y(m, c):
        return group([(tot.at[c * Y + 1 - y, m], yrecv.at[c, m], partner)], yrecv.at[c, m])

    y_waits = {(0, c): along_y(0, order[c]) for c in range(2)}
    keep(moments, keep_moments)
    wall[s] = weights[...] - 0.01 * (0.9 * moments[...])
    w_waits, w_y_waits = {}, []

    def along_z(k):
        w_waits[k] = group([(wall.at[s], wall.at[s], (((z + k) % Z) * Y + y, t))], wall.at[((z + Z - k) % Z) * Y + y])

    def own_to_partner():
        w_y_waits.append(group([(wall.at[s], wall.at[s], partner)], wall.at[z * Y + 1 - y]))

    def forward(k):
        c = (z + Z - k) % Z
        w_waits[k]()
        w_y_waits.append(group([(wall.at[c * Y + y], wall.at[c * Y + y], partner)], wall.at[c * Y + 1 - y]))

    def scatter_rows(i, part, square):
        for j in range(RANK // 8):
            scat[i, j] = part[8 * j : 8 * j + 8]
            scat[i, j + RANK // 8] = jnp.zeros((8, B), f32)
            if square is not None:
                scat[i, j + RANK // 8, :, 0:RANK] = square[8 * j : 8 * j + 8]
        return scatter_shard(scat.at[i], got.at[i])

    def gather_rows(i, wait):
        wait()
        piece = scat[i, s]
        for k in range(SHARD - 1):
            piece = piece + got[i, k]
        gath[i, s] = piece
        return spread_shard(gath.at[i])

    def rows_of(i, wait):
        wait()
        return gath[i, 0 : RANK // 8].reshape(RANK, B), gath[i, RANK // 8 : SHARD].reshape(RANK, B)[:, 0:RANK]

    along_z(1)
    part_o = nt(so[:, 0:B], tot[0, 1])
    for j in range(1, SHARD):
        part_o = part_o + nt(so[:, j * B : (j + 1) * B], tot[j, 1])
    o_wait = scatter_rows(0, part_o, None)
    for c in (2, 3):
        y_waits[0, c] = along_y(0, order[c])
    for c in range(Z):
        y_waits[1, c] = along_y(1, order[c])
    along_z(3)
    keep(tot, keep_tot)
    vec = grad_v[...].astype(f32)
    length = moment_v.shape[1]
    vpart[...] = jnp.zeros_like(vpart)
    vall[s] = jnp.zeros((1, VEC_PAD), f32)
    for j in range(SHARD):
        vpart[j, :, 0:length] = vec[:, j * length : (j + 1) * length]
    vector_wait = scatter_shard(vpart, vrecv)
    z_waits = {}
    for m in range(2):
        for k, c in enumerate(order[:3]):
            y_waits[m, k]()
            yrecv[c, m] = yrecv[c, m] + tot[c * Y + y, m]
            z_waits[m, k] = group([(yrecv.at[c, m], zrecv.at[k, m], (c * Y + y, t))], zrecv.at[k, m])
        if m == 0:
            o_wait = gather_rows(0, o_wait)

    def block(m):
        y_waits[m, 3]()
        total = yrecv[z, m] + tot[s, m]
        for k in range(Z - 1):
            z_waits[m, k]()
            total = total + zrecv[k, m]
        blk[m] = total

    def to_tensor_q(turn, factor):
        xq[turn, t] = nt(factor, blk[0])
        return spread_tensor(xq.at[turn])

    def to_tensor_o(turn, left):
        xo[turn, t, 0:RANK] = nn(left, blk[1])
        xo[turn, t, RANK : 2 * RANK] = jnp.zeros((RANK, B), f32)
        xo[turn, t, RANK : 2 * RANK, 0:RANK] = nt(left, left)
        return spread_tensor(xo.at[turn])

    def summed(ref, turn, wait):
        wait()
        return ref[turn, 0] + ref[turn, 1] + ref[turn, 2] + ref[turn, 3]

    own_to_partner()
    forward(1)
    block(0)
    xq_wait = to_tensor_q(0, sq[...])
    forward(3)
    vector_wait()
    vector_sum = vpart[s]
    for k in range(SHARD - 1):
        vector_sum = vector_sum + vrecv[k]
    moment = 0.9 * moment_v[...] + vector_sum[:, 0:length] / SHARD
    new_moment_v[...] = moment
    vall[s, :, 0:length] = weight_v[...] - 0.01 * moment
    left_q = summed(xq, 0, xq_wait)
    q_wait = scatter_rows(1, nn(left_q, blk[0]), nt(left_q, left_q))
    block(1)
    left_o, _ = rows_of(0, o_wait)
    xo_wait = to_tensor_o(0, left_o)
    q_wait = gather_rows(1, q_wait)
    vall_wait = spread_shard(vall)
    along_z(2)
    both = summed(xo, 0, xo_wait)
    factor_o, gram_o = both[0:RANK], both[RANK : 2 * RANK, 0:RANK]
    o_wait = scatter_rows(2, nt(factor_o, blk[1]), None)
    factor_q, gram_q = rows_of(1, q_wait)
    xq_wait = to_tensor_q(1, factor_q)
    o_wait = gather_rows(2, o_wait)
    forward(2)
    inverse_q, inverse_o = inverse_lower(gram_q), inverse_lower(gram_o)
    left_q = nn(inverse_q, summed(xq, 1, xq_wait))
    q_wait = scatter_rows(3, nn(left_q, blk[0]), nt(left_q, left_q))
    left_o = nn(inverse_o, rows_of(2, o_wait)[0])
    xo_wait = to_tensor_o(1, left_o)
    q_wait = gather_rows(3, q_wait)
    both = summed(xo, 1, xo_wait)
    factor_o, gram_o = both[0:RANK], both[RANK : 2 * RANK, 0:RANK]
    fall[s] = factor_o
    fall_wait = spread_shard(fall)
    pall[s] = left_q
    pall_wait = spread_shard(pall)
    factor_q, gram_q = rows_of(3, q_wait)
    inverse_q, inverse_o = inverse_lower(gram_q), inverse_lower(gram_o)
    side_q[...] = nn(inverse_q.T, nn(inverse_q, factor_q)) / SHARD
    side_o[...] = (nn(inverse_o.T, nn(inverse_o, left_o)) / SHARD).T
    keep(side_q, keep_q)
    keep(side_o, keep_o)
    for wait in w_y_waits:
        wait()
    keep(wall, keep_wall)
    vall_wait()
    keep(vall, keep_vall)
    pall_wait()
    keep(pall, keep_pall)
    fall_wait()
    keep(fall, keep_fall)
    for many, slot in sent:
        pltpu.make_async_copy(many, many, send_sem.at[slot]).wait()
    for copy in kept:
        copy.wait()


def finish(
    keep_tot, keep_wall, keep_pall, keep_fall, keep_q, keep_o, keep_moments, keep_vall, moment_v,
    new_error_q, new_error_o, new_moment_q, new_moment_o, new_weight_q, new_weight_o, new_moment_v, new_weight_v,
    tot, wall, pall, fall, side_q, side_o, moments, vall, eq, eo, mq, mo, wq, wo, sem, load_sem,
):
    pairs = (
        (keep_q, side_q), (keep_o, side_o), (keep_pall, pall), (keep_fall, fall), (keep_moments, moments),
        (keep_tot, tot), (keep_wall, wall), (keep_vall, vall),
    )
    loads = [pltpu.make_async_copy(src, dst, load_sem.at[i]) for i, (src, dst) in enumerate(pairs)]
    for load in loads:
        load.start()
    s = lax.axis_index("shard")
    out = []

    def leave(src, dst):
        copy = pltpu.make_async_copy(src, dst, sem.at[len(out)])
        copy.start()
        out.append(copy)

    for load in loads[:5]:
        load.wait()
    mq[...] = 0.9 * moments[0] + nn(pall[s].T, side_q[...])
    mo[...] = 0.9 * moments[1] + nn(side_o[...], fall[s])
    leave(mq, new_moment_q)
    leave(mo, new_moment_o)
    for load in loads[5:]:
        load.wait()
    for j in range(SHARD):
        rows = pl.ds(j * B, B)
        approx = nn(pall[j].T, side_q[...])
        eq[rows, :] = tot[j, 0] - approx
        wq[rows, :] = wall[j, 0] - 0.01 * approx
        approx = nn(side_o[...], fall[j])
        eo[:, rows] = tot[j, 1] - approx
        wo[:, rows] = wall[j, 1] - 0.01 * approx
        if j % 2:
            pair = pl.ds((j - 1) * B, 2 * B)
            leave(eq.at[pair, :], new_error_q.at[pair, :])
            leave(wq.at[pair, :], new_weight_q.at[pair, :])
            leave(eo.at[:, pair], new_error_o.at[:, pair])
            leave(wo.at[:, pair], new_weight_o.at[:, pair])
    length = moment_v.shape[1]
    new_moment_v[...] = moment_v[...]
    for j in range(SHARD):
        new_weight_v[:, j * length : (j + 1) * length] = vall[j, :, 0:length]
    for copy in out:
        copy.wait()


def fast_local(
    grad_query, error_query, grad_output, error_output, start_query, start_output, weight_query, weight_output,
    moment_query, moment_output, grad_vector, moment_vector, weight_vector,
):
    length = moment_vector.shape[0]
    vmem = pl.BlockSpec(memory_space=pltpu.VMEM)
    hbm = pl.BlockSpec(memory_space=pltpu.HBM)
    shape = lambda *dims: jax.ShapeDtypeStruct(dims, f32)
    scratch = lambda *dims: pltpu.VMEM(dims, f32)
    kept = pl.pallas_call(
        kernel,
        out_shape=(
            shape(SHARD, 2, B, B), shape(SHARD, 2, B, B), shape(SHARD, RANK, B), shape(SHARD, RANK, B),
            shape(RANK, B), shape(B, RANK), shape(2, B, B), shape(SHARD, 1, VEC_PAD), shape(1, length),
        ),
        in_specs=[hbm] * 10 + [vmem] * 3,
        out_specs=(hbm,) * 8 + (vmem,),
        scratch_shapes=[
            scratch(SHARD, 2, B, B), scratch(SHARD, 2, B, B), scratch(SHARD, RANK, B), scratch(SHARD, RANK, B),
            scratch(RANK, B), scratch(B, RANK), scratch(2, B, B), scratch(SHARD, 1, VEC_PAD),
            pltpu.VMEM((SHARD * B, B), grad_query.dtype), scratch(SHARD * B, B),
            pltpu.VMEM((B, SHARD * B), grad_output.dtype), scratch(B, SHARD * B),
            scratch(RANK, B), scratch(RANK, SHARD * B), scratch(2, B, B),
            scratch(Z, 2, B, B), scratch(Z - 1, 2, B, B), scratch(2, B, B),
            scratch(ROUNDS, TENSOR, RANK, B), scratch(ROUNDS, TENSOR, 2 * RANK, B),
            scratch(2 * ROUNDS, SHARD, 8, B), scratch(2 * ROUNDS, SHARD - 1, 8, B), scratch(2 * ROUNDS, SHARD, 8, B),
            scratch(SHARD, 1, VEC_PAD), scratch(SHARD - 1, 1, VEC_PAD),
            pltpu.SemaphoreType.DMA((SLOTS,)), pltpu.SemaphoreType.DMA((SLOTS,)), pltpu.SemaphoreType.DMA((10,)), pltpu.SemaphoreType.DMA((8,)),
        ],
        compiler_params=pltpu.CompilerParams(collective_id=0, has_side_effects=True, vmem_limit_bytes=60 * 2**20),
        cost_estimate=pl.CostEstimate(flops=2**30, bytes_accessed=5 * 2**20, transcendentals=0),
    )(
        grad_query[0], error_query[0], grad_output[0], error_output[0], start_query.T, start_output.T,
        weight_query, weight_output, moment_query, moment_output,
        grad_vector, moment_vector[None], weight_vector[None],
    )
    eq, eo, mq, mo, wq, wo, mv, wv = pl.pallas_call(
        finish,
        out_shape=(
            shape(SHARD * B, B), shape(B, SHARD * B), shape(B, B), shape(B, B),
            shape(SHARD * B, B), shape(B, SHARD * B), shape(1, length), shape(1, SHARD * length),
        ),
        in_specs=[hbm] * 8 + [vmem],
        out_specs=(hbm,) * 6 + (vmem,) * 2,
        scratch_shapes=[
            scratch(SHARD, 2, B, B), scratch(SHARD, 2, B, B), scratch(SHARD, RANK, B), scratch(SHARD, RANK, B),
            scratch(RANK, B), scratch(B, RANK), scratch(2, B, B), scratch(SHARD, 1, VEC_PAD),
            scratch(SHARD * B, B), scratch(B, SHARD * B), scratch(B, B), scratch(B, B),
            scratch(SHARD * B, B), scratch(B, SHARD * B), pltpu.SemaphoreType.DMA((2 + 2 * SHARD,)),
            pltpu.SemaphoreType.DMA((8,)),
        ],
        compiler_params=pltpu.CompilerParams(vmem_limit_bytes=60 * 2**20),
        cost_estimate=pl.CostEstimate(flops=2**26, bytes_accessed=5 * 2**20, transcendentals=0),
    )(*kept)
    return eq[None], eo[None], mq, mo, wq, wo, mv.reshape(-1), wv.reshape(-1)


def solution(mesh):
    in_specs = (
        P("shard", None, "tensor"),
        P("shard", None, "tensor"),
        P("shard", "tensor", None),
        P("shard", "tensor", None),
        P("tensor", None),
        P(),
        P("shard", "tensor"),
        P("tensor", "shard"),
        P("shard", "tensor"),
        P("tensor", "shard"),
        P("shard", None),
        P("shard"),
        P("shard"),
    )
    out_specs = (
        P("shard", None, "tensor"),
        P("shard", "tensor", None),
        P("shard", "tensor"),
        P("tensor", "shard"),
        P(None, "tensor"),
        P("tensor", None),
        P("shard"),
        P(),
    )
    body = fast_local if (mesh.shape["shard"], mesh.shape["tensor"]) == (Z * Y, TENSOR) else local
    return jax.shard_map(body, mesh=mesh, in_specs=in_specs, out_specs=out_specs, check_vma=False)
```

```python
import jax
import jax.numpy as jnp
from jax import lax
from jax.experimental import pallas as pl
from jax.experimental.pallas import tpu as pltpu
from jax.sharding import PartitionSpec as P

ROUNDS = 2


highest = lax.Precision.HIGHEST


def product(left, right):
    return jnp.dot(left, right, precision=highest, preferred_element_type=jnp.float32)


def product_inner(left, right):
    return lax.dot_general(
        left, right, (((0,), (0,)), ((), ())), precision=highest, preferred_element_type=jnp.float32
    )


def solve_rows(gram, factor):
    lower = jnp.linalg.cholesky(gram)
    return jax.scipy.linalg.solve_triangular(lower, factor.T, lower=True).T


def orthonormal(factor):
    return solve_rows(product_inner(factor, factor), factor)


def orthonormal_rows(factor):
    gram = lax.psum(product_inner(factor, factor), "tensor")
    return solve_rows(gram, factor)


def local(
    grad_query,
    error_query,
    grad_output,
    error_output,
    start_query,
    start_output,
    weight_query,
    weight_output,
    moment_query,
    moment_output,
    grad_vector,
    moment_vector,
    weight_vector,
):
    replicas = lax.axis_size("shard")
    shard_index = lax.axis_index("shard")
    total_query = grad_query[0].astype(jnp.float32) + error_query[0]
    total_output = grad_output[0].astype(jnp.float32) + error_output[0]
    factor_query = start_query
    factor_output = start_output
    for turn in range(ROUNDS):
        part_query = product(total_query, factor_query)
        part_output = product(total_output, factor_output)
        sum_query = lax.psum(part_query, ("shard", "tensor"))
        sum_output = lax.psum(part_output, "shard")
        left_query = orthonormal(sum_query)
        left_output = orthonormal_rows(sum_output)
        right_query_part = product_inner(total_query, left_query)
        right_output_part = product_inner(total_output, left_output)
        factor_query = lax.psum(right_query_part, "shard")
        factor_output = lax.psum(right_output_part, ("shard", "tensor"))
    approx_query = product(left_query, factor_query.T) / replicas
    approx_output = product(left_output, factor_output.T) / replicas
    new_error_query = (total_query - approx_query)[None]
    new_error_output = (total_output - approx_output)[None]
    rows_block = moment_query.shape[0]
    block_query = lax.dynamic_slice_in_dim(approx_query, shard_index * rows_block, rows_block, 0)
    cols_block = moment_output.shape[1]
    block_output = lax.dynamic_slice_in_dim(approx_output, shard_index * cols_block, cols_block, 1)
    new_moment_query = 0.9 * moment_query + block_query
    new_moment_output = 0.9 * moment_output + block_output
    stepped_query = weight_query - 0.01 * new_moment_query
    stepped_output = weight_output - 0.01 * new_moment_output
    local_vector = grad_vector[0].astype(jnp.float32)
    vector_block = moment_vector.shape[0]
    vector_whole = lax.psum(local_vector, "shard")
    vector_part = lax.dynamic_slice_in_dim(
        vector_whole, shard_index * vector_block, vector_block, 0
    )
    vector_mean = vector_part / replicas
    new_moment_vector = 0.9 * moment_vector + vector_mean
    stepped_vector = weight_vector - 0.01 * new_moment_vector
    new_weight_query, new_weight_output, new_weight_vector = (
        lax.all_gather(stepped_query, "shard", axis=0, tiled=True),
        lax.all_gather(stepped_output, "shard", axis=1, tiled=True),
        lax.all_gather(stepped_vector, "shard", axis=0, tiled=True),
    )
    return (
        new_error_query,
        new_error_output,
        new_moment_query,
        new_moment_output,
        new_weight_query,
        new_weight_output,
        new_moment_vector,
        new_weight_vector,
    )


Z, Y, TENSOR = 4, 2, 4
SHARD = Z * Y
RANK = 32
B = 128
VEC_PAD = 512
SLOTS = 64
f32 = jnp.float32


def nn(left, right):
    return lax.dot_general(left, right, (((1,), (0,)), ((), ())), precision=highest, preferred_element_type=f32)


def nt(left, right):
    return lax.dot_general(left, right, (((1,), (1,)), ((), ())), precision=highest, preferred_element_type=f32)


def inverse_lower(gram):
    row = lax.broadcasted_iota(jnp.int32, (RANK, RANK), 0)
    lane = lax.broadcasted_iota(jnp.int32, (RANK, RANK), 1)
    left, right = gram, (row == lane).astype(f32)
    for k in range(0, RANK, 2):
        first = jnp.broadcast_to(left[:, k : k + 1], (RANK, RANK))
        second = jnp.broadcast_to(left[:, k + 1 : k + 2], (RANK, RANK))
        over = 1.0 / first[k : k + 1]
        cross = first[k + 1 : k + 2]
        ratio = cross * over
        under = 1.0 / (second[k + 1 : k + 2] - cross * ratio)

        def reduced(matrix):
            top, low = matrix[k : k + 1], matrix[k + 1 : k + 2]
            low = (low - ratio * matrix[k : k + 1]) * under
            rest = first * (top * over - ratio * low) + second * low
            return matrix - jnp.where(row > k + 1, rest, jnp.where(row == k + 1, ratio * top, 0.0))

        left, right = reduced(left), reduced(right)
    diagonal = jnp.sum(jnp.where(row == lane, left, 0.0), axis=1, keepdims=True)
    return right * lax.rsqrt(diagonal)


def kernel(
    grad_q, error_q, grad_o, error_o, start_q, start_o, weight_q, weight_o, moment_q, moment_o,
    grad_v, moment_v, weight_v,
    keep_tot, keep_wall, keep_pall, keep_fall, keep_q, keep_o, keep_moments, keep_vall, new_moment_v,
    tot, wall, pall, fall, side_q, side_o, moments, vall, gq, eq, go, eo, sq, so, weights, yrecv, zrecv, blk, xq, xo, scat, got, gath, vpart, vrecv,
    send_sem, recv_sem, load_sem, keep_sem,
):
    s, t = lax.axis_index("shard"), lax.axis_index("tensor")
    z, y = s // Y, s % Y
    loads = [pltpu.make_async_copy(src, dst, load_sem.at[i])
             for i, (src, dst) in enumerate((
                 (grad_q, gq), (error_q, eq), (grad_o, go), (error_o, eo), (start_q, sq), (start_o, so),
                 (weight_q, weights.at[0]), (weight_o, weights.at[1]),
                 (moment_q, moments.at[0]), (moment_o, moments.at[1]),
             ))]
    for load in loads:
        load.start()
    barrier = pltpu.get_barrier_semaphore()
    for k in range(1, SHARD):
        pl.semaphore_signal(barrier, inc=1, device_id=((s + k) % SHARD, t), device_id_type=pl.DeviceIdType.MESH)
    for k in range(1, TENSOR):
        pl.semaphore_signal(barrier, inc=1, device_id=(s, (t + k) % TENSOR), device_id_type=pl.DeviceIdType.MESH)

    kept = []

    def keep(src, dst):
        copy = pltpu.make_async_copy(src, dst, keep_sem.at[len(kept)])
        copy.start()
        kept.append(copy)

    used = [0]
    sent = []

    def group(copies, many):
        slot = used[0]
        used[0] += 1
        for src, dst, device in copies:
            pltpu.make_async_remote_copy(
                src_ref=src, dst_ref=dst, send_sem=send_sem.at[slot], recv_sem=recv_sem.at[slot],
                device_id=device, device_id_type=pl.DeviceIdType.MESH).start()
        sent.append((many, slot))
        return lambda: pltpu.make_async_copy(many, many, recv_sem.at[slot]).wait()

    def spread_shard(buf):
        return group([(buf.at[s], buf.at[s], ((s + k) % SHARD, t)) for k in range(1, SHARD)], buf.at[pl.ds(0, SHARD - 1)])

    def spread_tensor(buf):
        return group([(buf.at[t], buf.at[t], (s, (t + k) % TENSOR)) for k in range(1, TENSOR)], buf.at[pl.ds(0, TENSOR - 1)])

    def scatter_shard(src, dst):
        return group([(src.at[(s + k) % SHARD], dst.at[k - 1], ((s + k) % SHARD, t)) for k in range(1, SHARD)], dst)

    for load in loads:
        load.wait()
    for j in range(SHARD):
        tot[j, 0] = gq[j * B : (j + 1) * B, :].astype(f32) + eq[j * B : (j + 1) * B, :]
        tot[j, 1] = go[:, j * B : (j + 1) * B].astype(f32) + eo[:, j * B : (j + 1) * B]
    pl.semaphore_wait(barrier, SHARD - 1 + TENSOR - 1)

    partner = (z * Y + 1 - y, t)
    order = [(z + k) % Z for k in (1, 2, 3, 0)]

    def along_y(m, c):
        return group([(tot.at[c * Y + 1 - y, m], yrecv.at[c, m], partner)], yrecv.at[c, m])

    y_waits = {(0, c): along_y(0, order[c]) for c in range(2)}
    keep(moments, keep_moments)
    wall[s] = weights[...] - 0.01 * (0.9 * moments[...])
    w_waits, w_y_waits = {}, []

    def along_z(k):
        w_waits[k] = group([(wall.at[s], wall.at[s], (((z + k) % Z) * Y + y, t))], wall.at[((z + Z - k) % Z) * Y + y])

    def own_to_partner():
        w_y_waits.append(group([(wall.at[s], wall.at[s], partner)], wall.at[z * Y + 1 - y]))

    def forward(k):
        c = (z + Z - k) % Z
        w_waits[k]()
        w_y_waits.append(group([(wall.at[c * Y + y], wall.at[c * Y + y], partner)], wall.at[c * Y + 1 - y]))

    def scatter_rows(i, part, square):
        for j in range(RANK // 8):
            scat[i, j] = part[8 * j : 8 * j + 8]
            scat[i, j + RANK // 8] = jnp.zeros((8, B), f32)
            if square is not None:
                scat[i, j + RANK // 8, :, 0:RANK] = square[8 * j : 8 * j + 8]
        return scatter_shard(scat.at[i], got.at[i])

    def gather_rows(i, wait):
        wait()
        piece = scat[i, s]
        for k in range(SHARD - 1):
            piece = piece + got[i, k]
        gath[i, s] = piece
        return spread_shard(gath.at[i])

    def rows_of(i, wait):
        wait()
        return gath[i, 0 : RANK // 8].reshape(RANK, B), gath[i, RANK // 8 : SHARD].reshape(RANK, B)[:, 0:RANK]

    along_z(2)
    part_o = nt(so[:, 0:B], tot[0, 1])
    for j in range(1, SHARD):
        part_o = part_o + nt(so[:, j * B : (j + 1) * B], tot[j, 1])
    o_wait = scatter_rows(0, part_o, None)
    for c in (2, 3):
        y_waits[0, c] = along_y(0, order[c])
    for c in range(Z):
        y_waits[1, c] = along_y(1, order[c])
    keep(tot, keep_tot)
    vec = grad_v[...].astype(f32)
    length = moment_v.shape[1]
    vpart[...] = jnp.zeros_like(vpart)
    vall[s] = jnp.zeros((1, VEC_PAD), f32)
    for j in range(SHARD):
        vpart[j, :, 0:length] = vec[:, j * length : (j + 1) * length]
    vector_wait = scatter_shard(vpart, vrecv)
    z_waits = {}
    for m in range(2):
        for k, c in enumerate(order[:3]):
            y_waits[m, k]()
            yrecv[c, m] = yrecv[c, m] + tot[c * Y + y, m]
            z_waits[m, k] = group([(yrecv.at[c, m], zrecv.at[k, m], (c * Y + y, t))], zrecv.at[k, m])
        if m == 0:
            o_wait = gather_rows(0, o_wait)

    def block(m):
        y_waits[m, 3]()
        total = yrecv[z, m] + tot[s, m]
        for k in range(Z - 1):
            z_waits[m, k]()
            total = total + zrecv[k, m]
        blk[m] = total

    def to_tensor_q(turn, factor):
        xq[turn, t] = nt(factor, blk[0])
        return spread_tensor(xq.at[turn])

    def to_tensor_o(turn, left):
        xo[turn, t, 0:RANK] = nn(left, blk[1])
        xo[turn, t, RANK : 2 * RANK] = jnp.zeros((RANK, B), f32)
        xo[turn, t, RANK : 2 * RANK, 0:RANK] = nt(left, left)
        return spread_tensor(xo.at[turn])

    def summed(ref, turn, wait):
        wait()
        return ref[turn, 0] + ref[turn, 1] + ref[turn, 2] + ref[turn, 3]

    own_to_partner()
    forward(2)
    block(0)
    xq_wait = to_tensor_q(0, sq[...])
    vector_wait()
    vector_sum = vpart[s]
    for k in range(SHARD - 1):
        vector_sum = vector_sum + vrecv[k]
    moment = 0.9 * moment_v[...] + vector_sum[:, 0:length] / SHARD
    new_moment_v[...] = moment
    vall[s, :, 0:length] = weight_v[...] - 0.01 * moment
    left_q = summed(xq, 0, xq_wait)
    q_wait = scatter_rows(1, nn(left_q, blk[0]), nt(left_q, left_q))
    block(1)
    left_o, _ = rows_of(0, o_wait)
    xo_wait = to_tensor_o(0, left_o)
    q_wait = gather_rows(1, q_wait)
    vall_wait = spread_shard(vall)
    along_z(1)
    both = summed(xo, 0, xo_wait)
    factor_o, gram_o = both[0:RANK], both[RANK : 2 * RANK, 0:RANK]
    o_wait = scatter_rows(2, nt(factor_o, blk[1]), None)
    factor_q, gram_q = rows_of(1, q_wait)
    xq_wait = to_tensor_q(1, factor_q)
    o_wait = gather_rows(2, o_wait)
    along_z(3)
    forward(1)
    inverse_q, inverse_o = inverse_lower(gram_q), inverse_lower(gram_o)
    left_q = nn(inverse_q, summed(xq, 1, xq_wait))
    q_wait = scatter_rows(3, nn(left_q, blk[0]), nt(left_q, left_q))
    left_o = nn(inverse_o, rows_of(2, o_wait)[0])
    xo_wait = to_tensor_o(1, left_o)
    q_wait = gather_rows(3, q_wait)
    both = summed(xo, 1, xo_wait)
    factor_o, gram_o = both[0:RANK], both[RANK : 2 * RANK, 0:RANK]
    fall[s] = factor_o
    fall_wait = spread_shard(fall)
    pall[s] = left_q
    pall_wait = spread_shard(pall)
    forward(3)
    inverse_o = inverse_lower(gram_o)
    factor_q, gram_q = rows_of(3, q_wait)
    inverse_q = inverse_lower(gram_q)
    side_q[...] = nn(inverse_q.T, nn(inverse_q, factor_q)) / SHARD
    side_o[...] = (nn(inverse_o.T, nn(inverse_o, left_o)) / SHARD).T
    keep(side_q, keep_q)
    keep(side_o, keep_o)
    for wait in w_y_waits:
        wait()
    keep(wall, keep_wall)
    vall_wait()
    keep(vall, keep_vall)
    pall_wait()
    keep(pall, keep_pall)
    fall_wait()
    keep(fall, keep_fall)
    for many, slot in sent:
        pltpu.make_async_copy(many, many, send_sem.at[slot]).wait()
    for copy in kept:
        copy.wait()


def finish(
    keep_tot, keep_wall, keep_pall, keep_fall, keep_q, keep_o, keep_moments, keep_vall, moment_v,
    new_error_q, new_error_o, new_moment_q, new_moment_o, new_weight_q, new_weight_o, new_moment_v, new_weight_v,
    tot, wall, pall, fall, side_q, side_o, moments, vall, eq, eo, mq, mo, wq, wo, sem, load_sem,
):
    pairs = (
        (keep_q, side_q), (keep_o, side_o), (keep_pall, pall), (keep_fall, fall), (keep_moments, moments),
        (keep_tot, tot), (keep_wall, wall), (keep_vall, vall),
    )
    loads = [pltpu.make_async_copy(src, dst, load_sem.at[i]) for i, (src, dst) in enumerate(pairs)]
    for load in loads:
        load.start()
    s = lax.axis_index("shard")
    out = []

    def leave(src, dst):
        copy = pltpu.make_async_copy(src, dst, sem.at[len(out)])
        copy.start()
        out.append(copy)

    for load in loads[:5]:
        load.wait()
    mq[...] = 0.9 * moments[0] + nn(pall[s].T, side_q[...])
    mo[...] = 0.9 * moments[1] + nn(side_o[...], fall[s])
    leave(mq, new_moment_q)
    leave(mo, new_moment_o)
    for load in loads[5:]:
        load.wait()
    for j in range(SHARD):
        rows = pl.ds(j * B, B)
        approx = nn(pall[j].T, side_q[...])
        eq[rows, :] = tot[j, 0] - approx
        wq[rows, :] = wall[j, 0] - 0.01 * approx
        approx = nn(side_o[...], fall[j])
        eo[:, rows] = tot[j, 1] - approx
        wo[:, rows] = wall[j, 1] - 0.01 * approx
        if j % 2:
            pair = pl.ds((j - 1) * B, 2 * B)
            leave(eq.at[pair, :], new_error_q.at[pair, :])
            leave(wq.at[pair, :], new_weight_q.at[pair, :])
            leave(eo.at[:, pair], new_error_o.at[:, pair])
            leave(wo.at[:, pair], new_weight_o.at[:, pair])
    length = moment_v.shape[1]
    new_moment_v[...] = moment_v[...]
    for j in range(SHARD):
        new_weight_v[:, j * length : (j + 1) * length] = vall[j, :, 0:length]
    for copy in out:
        copy.wait()


def fast_local(
    grad_query, error_query, grad_output, error_output, start_query, start_output, weight_query, weight_output,
    moment_query, moment_output, grad_vector, moment_vector, weight_vector,
):
    length = moment_vector.shape[0]
    vmem = pl.BlockSpec(memory_space=pltpu.VMEM)
    hbm = pl.BlockSpec(memory_space=pltpu.HBM)
    shape = lambda *dims: jax.ShapeDtypeStruct(dims, f32)
    scratch = lambda *dims: pltpu.VMEM(dims, f32)
    kept = pl.pallas_call(
        kernel,
        out_shape=(
            shape(SHARD, 2, B, B), shape(SHARD, 2, B, B), shape(SHARD, RANK, B), shape(SHARD, RANK, B),
            shape(RANK, B), shape(B, RANK), shape(2, B, B), shape(SHARD, 1, VEC_PAD), shape(1, length),
        ),
        in_specs=[hbm] * 10 + [vmem] * 3,
        out_specs=(hbm,) * 8 + (vmem,),
        scratch_shapes=[
            scratch(SHARD, 2, B, B), scratch(SHARD, 2, B, B), scratch(SHARD, RANK, B), scratch(SHARD, RANK, B),
            scratch(RANK, B), scratch(B, RANK), scratch(2, B, B), scratch(SHARD, 1, VEC_PAD),
            pltpu.VMEM((SHARD * B, B), grad_query.dtype), scratch(SHARD * B, B),
            pltpu.VMEM((B, SHARD * B), grad_output.dtype), scratch(B, SHARD * B),
            scratch(RANK, B), scratch(RANK, SHARD * B), scratch(2, B, B),
            scratch(Z, 2, B, B), scratch(Z - 1, 2, B, B), scratch(2, B, B),
            scratch(ROUNDS, TENSOR, RANK, B), scratch(ROUNDS, TENSOR, 2 * RANK, B),
            scratch(2 * ROUNDS, SHARD, 8, B), scratch(2 * ROUNDS, SHARD - 1, 8, B), scratch(2 * ROUNDS, SHARD, 8, B),
            scratch(SHARD, 1, VEC_PAD), scratch(SHARD - 1, 1, VEC_PAD),
            pltpu.SemaphoreType.DMA((SLOTS,)), pltpu.SemaphoreType.DMA((SLOTS,)), pltpu.SemaphoreType.DMA((10,)), pltpu.SemaphoreType.DMA((8,)),
        ],
        compiler_params=pltpu.CompilerParams(collective_id=0, has_side_effects=True, vmem_limit_bytes=60 * 2**20),
        cost_estimate=pl.CostEstimate(flops=2**30, bytes_accessed=5 * 2**20, transcendentals=0),
    )(
        grad_query[0], error_query[0], grad_output[0], error_output[0], start_query.T, start_output.T,
        weight_query, weight_output, moment_query, moment_output,
        grad_vector, moment_vector[None], weight_vector[None],
    )
    eq, eo, mq, mo, wq, wo, mv, wv = pl.pallas_call(
        finish,
        out_shape=(
            shape(SHARD * B, B), shape(B, SHARD * B), shape(B, B), shape(B, B),
            shape(SHARD * B, B), shape(B, SHARD * B), shape(1, length), shape(1, SHARD * length),
        ),
        in_specs=[hbm] * 8 + [vmem],
        out_specs=(hbm,) * 6 + (vmem,) * 2,
        scratch_shapes=[
            scratch(SHARD, 2, B, B), scratch(SHARD, 2, B, B), scratch(SHARD, RANK, B), scratch(SHARD, RANK, B),
            scratch(RANK, B), scratch(B, RANK), scratch(2, B, B), scratch(SHARD, 1, VEC_PAD),
            scratch(SHARD * B, B), scratch(B, SHARD * B), scratch(B, B), scratch(B, B),
            scratch(SHARD * B, B), scratch(B, SHARD * B), pltpu.SemaphoreType.DMA((2 + 2 * SHARD,)),
            pltpu.SemaphoreType.DMA((8,)),
        ],
        compiler_params=pltpu.CompilerParams(vmem_limit_bytes=60 * 2**20),
        cost_estimate=pl.CostEstimate(flops=2**26, bytes_accessed=5 * 2**20, transcendentals=0),
    )(*kept)
    return eq[None], eo[None], mq, mo, wq, wo, mv.reshape(-1), wv.reshape(-1)


def solution(mesh):
    in_specs = (
        P("shard", None, "tensor"),
        P("shard", None, "tensor"),
        P("shard", "tensor", None),
        P("shard", "tensor", None),
        P("tensor", None),
        P(),
        P("shard", "tensor"),
        P("tensor", "shard"),
        P("shard", "tensor"),
        P("tensor", "shard"),
        P("shard", None),
        P("shard"),
        P("shard"),
    )
    out_specs = (
        P("shard", None, "tensor"),
        P("shard", "tensor", None),
        P("shard", "tensor"),
        P("tensor", "shard"),
        P(None, "tensor"),
        P("tensor", None),
        P("shard"),
        P(),
    )
    body = fast_local if (mesh.shape["shard"], mesh.shape["tensor"]) == (Z * Y, TENSOR) else local
    return jax.shard_map(body, mesh=mesh, in_specs=in_specs, out_specs=out_specs, check_vma=False)
```
